32 devices in a mesh: dp: 8 (over z, y), tensor: 4 (over x, core).
Axes of the slice: x: 2, y: 2, z: 4, core: 2. Of those that a mesh axis runs over, the one named last changes fastest.
Arguments:
- hidden_in: float32 [16384, 1024], P('dp'), may hold values from -6 to 6
- seg_ids: int32 [8, 2048], P('dp'), may hold values from 0 to 3, never falling along the last dimension, each value on 1 to 1024 neighbouring positions
- token_mask: int32 [8, 2048], P('dp'), may hold values 0 or 1
- out_grad: float32 [16384, 1024], P('dp'), may hold values from -6 to 6
- proj_qkv: float32 [1024, 4096], P('dp', 'tensor'), may hold values from -0.1875 to 0.1875
- proj_out: float32 [2048, 1024], P('tensor', 'dp'), may hold values from -0.5 to 0.5
- proj_gate_up: float32 [1024, 6144], P('dp', 'tensor'), may hold values from -0.1875 to 0.1875
- proj_down: float32 [3072, 1024], P('tensor', 'dp'), may hold values from -0.109375 to 0.109375
- gains: float32 [2304], replicated, may hold values from 0.5 to 1.5
- moment_qkv: float32 [1024, 4096], P('dp', 'tensor'), may hold values from -28 to 28
- moment_out: float32 [2048, 1024], P('tensor', 'dp'), may hold values from -28 to 28
- moment_gate_up: float32 [1024, 6144], P('dp', 'tensor'), may hold values from -28 to 28
- moment_down: float32 [3072, 1024], P('tensor', 'dp'), may hold values from -28 to 28
- error_qkv: float32 [8, 1024, 4096], P('dp', None, 'tensor'), may hold values from -80 to 80
- error_out: float32 [8, 2048, 1024], P('dp', 'tensor'), may hold values from -80 to 80
- error_gate_up: float32 [8, 1024, 6144], P('dp', None, 'tensor'), may hold values from -80 to 80
- error_down: float32 [8, 3072, 1024], P('dp', 'tensor'), may hold values from -80 to 80
- factor_qkv: float32 [4096, 8], P('tensor'), may hold values from -6 to 6
- factor_out: float32 [2048, 8], P('tensor'), may hold values from -6 to 6
- factor_gate_up: float32 [6144, 8], P('tensor'), may hold values from -6 to 6
- factor_down: float32 [3072, 8], P('tensor'), may hold values from -6 to 6
- gain_moment: float32 [2304], replicated, may hold values from -48 to 48
Outputs:
- layer_out: float32 [16384, 1024], P('dp')
- input_grad: float32 [16384, 1024], P('dp')
- new_proj_qkv: float32 [1024, 4096], P('dp', 'tensor')
- new_proj_out: float32 [2048, 1024], P('tensor', 'dp')
- new_proj_gate_up: float32 [1024, 6144], P('dp', 'tensor')
- new_proj_down: float32 [3072, 1024], P('tensor', 'dp')
- new_moment_qkv: float32 [1024, 4096], P('dp', 'tensor')
- new_moment_out: float32 [2048, 1024], P('tensor', 'dp')
- new_moment_gate_up: float32 [1024, 6144], P('dp', 'tensor')
- new_moment_down: float32 [3072, 1024], P('tensor', 'dp')
- new_error_qkv: float32 [8, 1024, 4096], P('dp', None, 'tensor')
- new_error_out: float32 [8, 2048, 1024], P('dp', 'tensor')
- new_error_gate_up: float32 [8, 1024, 6144], P('dp', None, 'tensor')
- new_error_down: float32 [8, 3072, 1024], P('dp', 'tensor')
- new_factor_qkv: float32 [4096, 8], P('tensor')
- new_factor_out: float32 [2048, 8], P('tensor')
- new_factor_gate_up: float32 [6144, 8], P('tensor')
- new_factor_down: float32 [3072, 8], P('tensor')
- new_gains: float32 [2304], replicated
- new_gain_moment: float32 [2304], replicated
The draws below stay inside these ranges and needn't reach their ends.
Inputs may be any that keep to these rules, and one draw needn't show every extreme that they name: `seg_ids`: segment numbers never fall along a sequence; a document has at most 1024 tokens.
All inputs are finite; a program needn't handle non-finite values. No bound on the sum of `token_mask` on one device may be relied on, other than what follows from the above.
Results may differ from the reference program's by a relative error of at most 0.018.
The reference program's roundings to bfloat16 on the way count: a program that leaves them out, or rounds other values in their place, can miss the bound.
Values may be sent and summed in bfloat16 or wider, within the bound.
No kernel may reach another device: no remote copies, remote signals or barrier semaphores. Data moves between devices by JAX's collectives and lax.ppermute only.
A program may use at most 256 MiB of HBM per device.

```python
import math
import jax
import jax.numpy as jnp
import numpy as np
from jax import lax

D = 1024
QUERY_HEADS = 16
KEY_VALUE_HEADS = 8
HEAD_SIZE = 128
FF = 3072
RANK = 8
TOK_DEV = 2048
SEQS = 8
TOKENS = 16384
QKV_COLS = 4096
QUERY_HEAD_WIDTH = 2048
GAINS = 2304
N_DP = 8
N_TENSOR = 4


def place_ends(array, key, least, top_value):
    dims = array.shape
    place = [jax.random.randint(jax.random.fold_in(key, axis), (), 0, dims[axis]) for axis in range(len(dims))]
    array = array.at[tuple(place)].set(least)
    longest = dims.index(max(dims))
    place[longest] = (place[longest] + 1) % dims[longest]
    return array.at[tuple(place)].set(top_value)


def steps_of(own_key, dims, shards, low, top_value):
    def one(dim, parts):
        heights = jax.random.uniform(jax.random.fold_in(jax.random.fold_in(own_key, 6), dim), (parts,), jnp.float32, low / len(shards), top_value / len(shards))
        return jnp.repeat(jnp.exp(heights), dims[dim] // parts).reshape((-1,) + (1,) * (len(dims) - dim - 1))

    gain = one(*shards[0])
    for cut in shards[1:]:
        gain = gain * one(*cut)
    return gain


def length_profile(number_of, total, reach, skew):
    weights = [(1 << 20) // math.isqrt(standing ** skew) + 1 for standing in range(2, number_of + 1)]
    surplus, counts = total - reach - (number_of - 1), [1] * (number_of - 1)
    while surplus > 0:
        candidates = [i for i in range(number_of - 1) if counts[i] < reach]
        pool, left = sum([weights[i] for i in candidates]), surplus
        for i in candidates:
            more = min(reach - counts[i], max(1, left * weights[i] // pool), surplus)
            counts[i] = counts[i] + more
            surplus = surplus - more
    return np.array([reach] + counts)


def ragged_sizes(own_key, number_of, total, bound, skew):
    if number_of == 2:
        one = jax.random.randint(own_key, (), max(1, total - bound), min(bound, total - 1) + 1)
        return jnp.stack([one, total - one])
    tallies = jnp.asarray(length_profile(number_of, total, bound, skew), jnp.int32)
    couples = (number_of - 1) // 2
    donor, taker = tallies[1:1 + 2 * couples:2], tallies[2:2 + 2 * couples:2]
    room = jnp.minimum(donor - 1, bound - taker)
    moved = jax.random.randint(jax.random.fold_in(own_key, 1), (couples,), 0, 1 << 20) % (room + 1)
    tallies = tallies.at[1:1 + 2 * couples:2].set(donor - moved).at[2:2 + 2 * couples:2].set(taker + moved)
    return tallies[jax.random.permutation(jax.random.fold_in(own_key, 2), number_of)]


def bell_draw(rng, dims, scale, reach, pieces=(), held_as=jnp.bfloat16):
    values = jax.random.normal(rng, dims, jnp.float32) * scale
    if len(pieces) > 0:
        values = steps_of(rng, dims, pieces, -0.22, 0.18) * values
    return jnp.clip(values, min=-reach, max=reach).astype(held_as)


def setup_inputs(seed: int = 0) -> dict:
    streams_of = jax.random.split(jax.random.key(seed), 23)
    hidden_in = bell_draw(streams_of[0], (TOKENS, D), 1.0, 6.0, ((0, 8),), jnp.float32)
    seg_ids = jax.vmap(lambda own: jnp.searchsorted(jnp.cumsum(ragged_sizes(own, 4, TOK_DEV, TOK_DEV // 2, 1)), jnp.arange(TOK_DEV), side="right"))(jax.random.split(streams_of[1], SEQS)).reshape((SEQS, TOK_DEV)).astype(jnp.int32)
    token_mask = place_ends((jax.random.randint(streams_of[2], (SEQS, TOK_DEV), 0, 8) < 7).astype(jnp.int32), jax.random.fold_in(streams_of[2], 1), 0, 1)
    out_grad = bell_draw(streams_of[3], (TOKENS, D), 1.0, 6.0, ((0, 8),), jnp.float32)
    proj_qkv = bell_draw(streams_of[4], (D, QKV_COLS), D ** -0.5, 0.1875, ((0, 8), (1, 4)), jnp.float32)
    proj_out = bell_draw(streams_of[5], (QUERY_HEAD_WIDTH, D), (QUERY_HEAD_WIDTH // 16) ** -0.5, 0.5, ((0, 4), (1, 8)), jnp.float32)
    proj_gate_up = bell_draw(streams_of[6], (D, 2 * FF), D ** -0.5, 0.1875, ((0, 8), (1, 4)), jnp.float32)
    proj_down = bell_draw(streams_of[7], (FF, D), FF ** -0.5, 0.109375, ((0, 4), (1, 8)), jnp.float32)
    gains = jnp.clip(1.0 + 0.1 * jax.random.normal(streams_of[8], (GAINS,), jnp.float32), 0.5, 1.5)
    moment_qkv = bell_draw(streams_of[9], (D, QKV_COLS), (0.1 * TOK_DEV ** 0.5), 28.0, ((0, 8), (1, 4)), jnp.float32)
    moment_out = bell_draw(streams_of[10], (QUERY_HEAD_WIDTH, D), (0.1 * TOK_DEV ** 0.5), 28.0, ((0, 4), (1, 8)), jnp.float32)
    moment_gate_up = bell_draw(streams_of[11], (D, 2 * FF), (0.1 * TOK_DEV ** 0.5), 28.0, ((0, 8), (1, 4)), jnp.float32)
    moment_down = bell_draw(streams_of[12], (FF, D), (0.1 * TOK_DEV ** 0.5), 28.0, ((0, 4), (1, 8)), jnp.float32)
    error_qkv = bell_draw(streams_of[13], (SEQS, D, QKV_COLS), (0.3 * TOK_DEV ** 0.5), 80.0, ((0, 8), (2, 4)), jnp.float32)
    error_out = bell_draw(streams_of[14], (SEQS, QUERY_HEAD_WIDTH, D), (0.3 * TOK_DEV ** 0.5), 80.0, ((0, 8), (1, 4)), jnp.float32)
    error_gate_up = bell_draw(streams_of[15], (SEQS, D, 2 * FF), (0.3 * TOK_DEV ** 0.5), 80.0, ((0, 8), (2, 4)), jnp.float32)
    error_down = bell_draw(streams_of[16], (SEQS, FF, D), (0.3 * TOK_DEV ** 0.5), 80.0, ((0, 8), (1, 4)), jnp.float32)
    factor_qkv = bell_draw(streams_of[17], (QKV_COLS, RANK), 1.0, 6.0, ((0, 4),), jnp.float32)
    factor_out = bell_draw(streams_of[18], (QUERY_HEAD_WIDTH, RANK), 1.0, 6.0, ((0, 4),), jnp.float32)
    factor_gate_up = bell_draw(streams_of[19], (2 * FF, RANK), 1.0, 6.0, ((0, 4),), jnp.float32)
    factor_down = bell_draw(streams_of[20], (FF, RANK), 1.0, 6.0, ((0, 4),), jnp.float32)
    gain_moment = bell_draw(streams_of[21], (GAINS,), (0.5 * (TOK_DEV // SEQS + 1) ** 0.5), 48.0, (), jnp.float32)
    return dict(hidden_in=hidden_in, seg_ids=seg_ids, token_mask=token_mask, out_grad=out_grad, proj_qkv=proj_qkv, proj_out=proj_out, proj_gate_up=proj_gate_up, proj_down=proj_down, gains=gains, moment_qkv=moment_qkv, moment_out=moment_out, moment_gate_up=moment_gate_up, moment_down=moment_down, error_qkv=error_qkv, error_out=error_out, error_gate_up=error_gate_up, error_down=error_down, factor_qkv=factor_qkv, factor_out=factor_out, factor_gate_up=factor_gate_up, factor_down=factor_down, gain_moment=gain_moment)


EPSILON = 1e-06
ROPE_THETA = 1000000.0
MASKED = -1000000000.0
MOMENTUM = 0.5
STEP_RATE = 0.003
GAIN_RATE = 0.02
EXACT_PRECISION = lax.Precision.HIGHEST

@jax.custom_vjp
def lowered_factor(v):
    return lax.optimization_barrier(v.astype(jnp.bfloat16)).astype(jnp.float32)

@jax.custom_vjp
def lowered_return(v):
    return v

def low_keep(v):
    return (lowered_factor(v), None)

def low_pass(kept, grad):
    return (grad,)

def back_keep(v):
    return (v, None)

def back_low(kept, grad):
    return (lowered_factor(grad),)
lowered_factor.defvjp(low_keep, low_pass)
lowered_return.defvjp(back_keep, back_low)

def matmul_hi(left, right):
    return jnp.dot(left, right, precision=EXACT_PRECISION, preferred_element_type=jnp.float32)

def row_root_means(values, gain_vec):
    return values * lax.rsqrt(lax.optimization_barrier(jnp.mean(values * values, axis=-1, keepdims=True)) + EPSILON) * gain_vec

def rope_tables(sequence_length):
    position = jnp.arange(sequence_length, dtype=jnp.float32)
    inverse = ROPE_THETA ** (-(jnp.arange(HEAD_SIZE // 2, dtype=jnp.float32) * 2.0 / HEAD_SIZE))
    angles = position[:, None] * inverse[None, :]
    return (jnp.cos(angles)[:, None, :], jnp.sin(angles)[:, None, :])

def apply_rotary(values, cosine_table, sine_table):
    half_dim = values.shape[-1] // 2
    first_half = values[..., :half_dim]
    second_half = values[..., half_dim:]
    return jnp.concatenate([first_half * cosine_table - second_half * sine_table, second_half * cosine_table + first_half * sine_table], axis=-1)

def layer(values, qkv_mat, out_mat, gu_mat, down_mat, gain_vec, seg_row, keep_row):
    sequence_length = values.shape[0]
    g_att = gain_vec[:D]
    g_mlp = gain_vec[D:2 * D]
    query_gradient = gain_vec[2 * D:2 * D + HEAD_SIZE]
    g_key = gain_vec[2 * D + HEAD_SIZE:]
    query_columns = QUERY_HEADS * HEAD_SIZE // N_TENSOR
    key_value_columns = KEY_VALUE_HEADS * HEAD_SIZE // N_TENSOR
    ff_cols = FF // N_TENSOR
    heads_per_group = QUERY_HEADS // KEY_VALUE_HEADS
    h_att = lowered_factor(row_root_means(values, g_att))
    unrotated_projection = lowered_return(matmul_hi(h_att, lowered_factor(qkv_mat))).reshape(sequence_length, N_TENSOR, QKV_COLS // N_TENSOR)
    unrotated_query = unrotated_projection[:, :, :query_columns].reshape(sequence_length, QUERY_HEADS, HEAD_SIZE)
    unrotated_key = unrotated_projection[:, :, query_columns:query_columns + key_value_columns].reshape(sequence_length, KEY_VALUE_HEADS, HEAD_SIZE)
    value_head_rows = lowered_factor(unrotated_projection[:, :, query_columns + key_value_columns:].reshape(sequence_length, KEY_VALUE_HEADS, HEAD_SIZE))
    cosine_table, sine_table = rope_tables(sequence_length)
    query_rows = lowered_factor(apply_rotary(row_root_means(unrotated_query, query_gradient), cosine_table, sine_table)).reshape(sequence_length, KEY_VALUE_HEADS, heads_per_group, HEAD_SIZE)
    key_head_rows = lowered_factor(apply_rotary(row_root_means(unrotated_key, g_key), cosine_table, sine_table))
    attention_scale = 1.0 / math.sqrt(HEAD_SIZE)
    attention_scores = lowered_return(jnp.einsum('cwbn,zwn->wbcz', query_rows, key_head_rows, precision=EXACT_PRECISION) * attention_scale)
    row_ids = jnp.arange(sequence_length)
    allowed = (row_ids[None, :] <= row_ids[:, None]) & (seg_row[None, :] == seg_row[:, None])
    allowed = allowed & ((keep_row[None, :] == 1) | (row_ids[None, :] == row_ids[:, None]))
    attention_scores = jnp.where(allowed, attention_scores, MASKED)
    row_max = lax.optimization_barrier(jnp.max(attention_scores, axis=-1, keepdims=True))
    expo_vals = jnp.exp(attention_scores - row_max)
    probabilities = expo_vals / lax.optimization_barrier(jnp.sum(expo_vals, axis=-1, keepdims=True))
    attention_output = jnp.einsum('ynel,lyf->eynf', lowered_factor(probabilities), value_head_rows, precision=EXACT_PRECISION).reshape(sequence_length, QUERY_HEAD_WIDTH)
    attention_output = lowered_factor(lowered_return(attention_output))
    branch_att = lowered_return(matmul_hi(attention_output, lowered_factor(out_mat)))
    resid_mid = values + branch_att
    h_mlp = lowered_factor(row_root_means(resid_mid, g_mlp))
    gate_up = lowered_return(matmul_hi(h_mlp, lowered_factor(gu_mat))).reshape(sequence_length, N_TENSOR, 2 * ff_cols)
    activ = lowered_factor((jax.nn.silu(gate_up[:, :, :ff_cols]) * gate_up[:, :, ff_cols:]).reshape(sequence_length, FF))
    branch_mlp = lowered_return(matmul_hi(activ, lowered_factor(down_mat)))
    return resid_mid + branch_mlp

def orthonormal(block):
    columns = []
    for column_id in range(block.shape[-1]):
        column = block[..., column_id]
        for finished in columns:
            column = column - lax.optimization_barrier(jnp.sum(column * finished, axis=-1, keepdims=True)) * finished
        column = column * lax.rsqrt(lax.optimization_barrier(jnp.sum(column * column, axis=-1, keepdims=True)) + 1e-12)
        columns.append(column)
    return jnp.stack(columns, axis=-1)

def compress(grads, errors, factor, moment, weight, flipped):
    merged = grads + errors
    oriented = jnp.swapaxes(merged, 1, 2) if flipped else merged
    workers = oriented.shape[0]
    cols_all = oriented.shape[2]
    split_cols = oriented.reshape(workers, D, N_TENSOR, cols_all // N_TENSOR)
    start_factor = factor.reshape(N_TENSOR, cols_all // N_TENSOR, RANK)
    p_mean = jnp.einsum('wdtc,tcr->tdr', split_cols, start_factor, precision=EXACT_PRECISION) / N_DP
    p_hat = orthonormal(p_mean)
    q_mean = jnp.einsum('wdtc,tdr->tcr', split_cols, p_hat, precision=EXACT_PRECISION) / N_DP
    approx = jnp.einsum('tdr,tcr->dtc', p_hat, q_mean, precision=EXACT_PRECISION).reshape(D, cols_all)
    approx = approx.T if flipped else approx
    new_moment = MOMENTUM * moment + approx
    new_weight = weight - STEP_RATE * new_moment
    return (new_weight, new_moment, merged - approx[None], q_mean.reshape(cols_all, RANK))

def reference(hidden_in, seg_ids, token_mask, out_grad, proj_qkv, proj_out, proj_gate_up, proj_down, gains, moment_qkv, moment_out, moment_gate_up, moment_down, error_qkv, error_out, error_gate_up, error_down, factor_qkv, factor_out, factor_gate_up, factor_down, gain_moment):
    seq_inputs = hidden_in.reshape(SEQS, TOK_DEV, D)
    seq_grads = out_grad.reshape(SEQS, TOK_DEV, D)

    def one_sequence(seq_item):
        seq_in, seq_grad, seg_row, keep_row = seq_item

        def layer_fn(values, qkv_mat, out_mat, gu_mat, down_mat, gain_vec):
            return layer(values, qkv_mat, out_mat, gu_mat, down_mat, gain_vec, seg_row, keep_row)
        result, pull_back = jax.vjp(layer_fn, seq_in, proj_qkv, proj_out, proj_gate_up, proj_down, gains)
        return (result,) + tuple(pull_back(seq_grad))
    results = lax.map(one_sequence, (seq_inputs, seq_grads, seg_ids, token_mask))
    layer_out = results[0].reshape(TOKENS, D)
    input_grad = results[1].reshape(TOKENS, D)
    gain_grad = lax.optimization_barrier(jnp.sum(results[6], axis=0)) / N_DP
    new_gain_moment = MOMENTUM * gain_moment + gain_grad
    new_gains = gains - GAIN_RATE * new_gain_moment
    out_qkv = compress(results[2], error_qkv, factor_qkv, moment_qkv, proj_qkv, False)
    out_att = compress(results[3], error_out, factor_out, moment_out, proj_out, True)
    out_gu = compress(results[4], error_gate_up, factor_gate_up, moment_gate_up, proj_gate_up, False)
    out_down = compress(results[5], error_down, factor_down, moment_down, proj_down, True)
    return (layer_out, input_grad, out_qkv[0], out_att[0], out_gu[0], out_down[0], out_qkv[1], out_att[1], out_gu[1], out_down[1], out_qkv[2], out_att[2], out_gu[2], out_down[2], out_qkv[3], out_att[3], out_gu[3], out_down[3], new_gains, new_gain_moment)
```

```python
import functools
import math

import jax
import jax.numpy as jnp
from jax import lax
from jax.experimental import pallas as pl
from jax.experimental.pallas import tpu as pltpu
from jax.sharding import PartitionSpec as P

D = 1024
QUERY_HEADS = 16
KEY_VALUE_HEADS = 8
HEAD_SIZE = 128
FF = 3072
RANK = 8


EPSILON = 1e-06
ROPE_THETA = 1000000.0
MOMENTUM = 0.5
STEP_RATE = 0.003
GAIN_RATE = 0.02
CHUNKS = 2
BLOCK = 256
ROWS = 256
SCALE = 1.0 / math.sqrt(HEAD_SIZE)
SCALE_2 = SCALE / math.log(2.0)
MIB = 1024 * 1024

HALF = jnp.bfloat16
FULL = jnp.float32
NN = (((1,), (0,)), ((), ()))
NT = (((1,), (1,)), ((), ()))
TN = (((0,), (0,)), ((), ()))


def mul(left, right, dims=NN):
    return lax.dot_general(left, right, dims, preferred_element_type=FULL)


def shape_of(dims, dtype):
    return jax.ShapeDtypeStruct(dims, dtype)


def far(array):
    return pltpu.with_memory_space_constraint(array, pltpu.HBM)


def near(array):
    return pltpu.with_memory_space_constraint(array, pltpu.VMEM)


def near_shape(dims, dtype):
    return pltpu.VMEM(dims, dtype)


def far_shape(dims, dtype):
    return pltpu.HBM(dims, dtype)


def whole(*dims):
    return pl.BlockSpec(dims, lambda *_: (0,) * len(dims), pipeline_mode=pl.Buffered(1))


def made(*dims):
    return pl.BlockSpec(dims, lambda *_: (0,) * len(dims))


def block_bytes(spec, array):
    if spec.block_shape is None:
        return 0
    size = array.dtype.itemsize
    *lead, height, width = spec.block_shape
    height = -(-height // (32 // size)) * (32 // size)
    count = 2 if spec.pipeline_mode is None else spec.pipeline_mode.buffer_count
    return math.prod(lead) * height * (-(-width // 128) * 128) * size * count


def call(kernel, grid, in_specs, out_specs, out_shape, args, scratch=(), table=None, flops=0, aliases=None, after=(), room=6):
    moved = sum(math.prod(a.shape) * a.dtype.itemsize for a in list(args) + list(out_shape))
    prefetch = () if table is None else (table,)
    first = len(prefetch) + len(args)
    need = sum(block_bytes(*pair) for pair in zip(list(in_specs) + list(out_specs), list(args) + list(out_shape)))
    need += sum(math.prod(item.shape) * jnp.dtype(item.dtype).itemsize for item in scratch) + room * MIB

    def body(*refs):
        kernel(*refs[:first], *refs[first + len(after) :])

    return pl.pallas_call(
        body,
        grid_spec=pltpu.PrefetchScalarGridSpec(
            num_scalar_prefetch=len(prefetch),
            grid=grid,
            in_specs=list(in_specs) + [pl.BlockSpec(memory_space=pl.ANY)] * len(after),
            out_specs=out_specs,
            scratch_shapes=list(scratch),
        ),
        out_shape=out_shape,
        input_output_aliases=aliases or {},
        compiler_params=pltpu.CompilerParams(vmem_limit_bytes=need),
        cost_estimate=pl.CostEstimate(
            flops=int(flops), bytes_accessed=int(moved), transcendentals=0
        ),
    )(*prefetch, *args, *after)


def rms_parts(values, gain_vec):
    factor = lax.rsqrt(jnp.mean(values * values, axis=-1, keepdims=True) + EPSILON)
    normal = values * factor
    return (normal * gain_vec, normal, factor)


def norm_back(grad_in, normal, factor, gain_vec):
    scaled = grad_in * gain_vec
    return factor * (scaled - normal * jnp.mean(scaled * normal, axis=-1, keepdims=True))


def rope_tables(sequence_length):
    position = jnp.arange(sequence_length, dtype=FULL)
    inverse = ROPE_THETA ** (-(jnp.arange(HEAD_SIZE // 2, dtype=FULL) * 2.0 / HEAD_SIZE))
    angles = position[:, None] * inverse[None, :]
    cosine, sine = jnp.cos(angles), jnp.sin(angles)
    return jnp.concatenate([cosine, cosine], 1), jnp.concatenate([-sine, sine], 1)


def ring_of(count):
    return list(range(0, count, 2)) + list(range(1, count, 2))[::-1]


def ring_step(pair, count, cut=None):
    ring = ring_of(count)
    ahead = [(ring[i], ring[(i + 1) % count]) for i in range(count)]
    back = [(target, source) for source, target in ahead]
    from_left, from_right = pair
    if cut is not None:
        from_left, from_right = from_left[:cut], from_right[cut:]
    return lax.ppermute(from_left, "dp", ahead), lax.ppermute(from_right, "dp", back)


def ring_gather(own, count):
    steps, pair = [], (own, own)
    for _ in range(count // 2 - 1):
        pair = ring_step(pair, count)
        steps.append(pair)
    steps.append(ring_step(pair, count, own.shape[0] // 2))
    return [own] + [piece for step in steps for piece in step], steps


def ring_places(count, shard):
    index = lax.axis_index("dp")
    here = jnp.where(index % 2 == 0, index // 2, count - 1 - index // 2)
    shifts = [0]
    for shift in range(1, count // 2):
        shifts += [count - shift, shift]
    shifts = jnp.array(shifts + [count // 2] * 2, jnp.int32)
    at = (here + shifts) % count
    owner = jnp.where(at < count // 2, 2 * at, 2 * (count - 1 - at) + 1)
    late = (jnp.arange(shifts.shape[0]) == shifts.shape[0] - 1).astype(jnp.int32)
    return (owner * shard + late * (shard // 2)).astype(jnp.int32)


def assemble(tab_ref, first, pieces, target):
    for number, piece in enumerate(pieces):
        rows = piece.shape[0]
        target[pl.ds(pl.multiple_of(tab_ref[first + number], rows), rows), :] = piece[...]


def stage_kernel(in_ref, out_ref):
    out_ref[...] = in_ref[...]


def stage(values, after):
    spec = whole(*values.shape)
    return call(stage_kernel, (1,), [spec], [made(*values.shape)], [shape_of(values.shape, values.dtype)], (values,), after=after)[0]


def input_kernel(x_ref, g_ref, h_ref):
    h_ref[...] = rms_parts(x_ref[...], g_ref[...])[0].astype(HALF)


def input_norm(hidden_in, g_att):
    rows = hidden_in.shape[0]
    by_row = pl.BlockSpec((BLOCK, D), lambda i: (i, 0))
    return call(
        input_kernel, (rows // BLOCK,), [by_row, whole(1, D)], [by_row], [shape_of((rows, D), HALF)],
        (far(hidden_in), g_att[None]),
    )[0]


def turn_kernel(h_ref, ht_ref):
    ht_ref[...] = h_ref[...].T


def turned(h_att, after):
    rows = h_att.shape[0]
    return call(
        turn_kernel,
        (rows // BLOCK,),
        [pl.BlockSpec((BLOCK, D), lambda i: (i, 0))],
        [pl.BlockSpec((D, BLOCK), lambda i: (0, i))],
        [far_shape((D, rows), HALF)],
        (h_att,),
        after=after,
    )[0]


def qkv_kernel(q_heads, kv_heads, count, tab_ref, h_ref, gq_ref, gk_ref, cos_ref, sin_ref, *refs):
    pieces, (w_ref, q_ref, k_ref, v_ref, kt_ref, rq_ref, rk_ref) = refs[:count], refs[count:]

    @pl.when(pl.program_id(0) == 0)
    def _():
        assemble(tab_ref, 0, pieces, w_ref)

    h_att = h_ref[...]
    cosine, sine = cos_ref[...], sin_ref[...]
    ones = jnp.ones((h_att.shape[0], HEAD_SIZE), HALF)
    for pair in range((q_heads + 2 * kv_heads) // 2):
        both = mul(h_att, w_ref[:, 2 * pair * HEAD_SIZE : 2 * (pair + 1) * HEAD_SIZE])
        for part in range(2):
            head = 2 * pair + part
            raw = both[:, heads_of(part)]
            if head >= q_heads + kv_heads:
                at = 2 * (head - q_heads - kv_heads) * HEAD_SIZE
                v_ref[:, at : at + HEAD_SIZE] = raw.astype(HALF)
                v_ref[:, at + HEAD_SIZE : at + 2 * HEAD_SIZE] = ones
                continue
            normed = rms_parts(raw, gq_ref[...] if head < q_heads else gk_ref[...])[0]
            rotated = normed * cosine + pltpu.roll(normed, HEAD_SIZE // 2, 1) * sine
            if head < q_heads:
                rq_ref[:, heads_of(head)] = raw
                q_ref[:, heads_of(head)] = rotated.astype(HALF)
            else:
                rk_ref[:, heads_of(head - q_heads)] = raw
                k_ref[:, heads_of(head - q_heads)] = rotated.astype(HALF)
                kt_ref[heads_of(head - q_heads), :] = rotated.T.astype(HALF)


def make_qkv(table, h_att, pieces, g_query, g_key, cosine, sine, q_heads, kv_heads, after):
    rows = h_att.shape[0]
    q_cols, k_cols = q_heads * HEAD_SIZE, kv_heads * HEAD_SIZE
    cols = q_cols + 2 * k_cols
    w_cols = pieces[0].shape[1]
    by_row = lambda width: pl.BlockSpec((BLOCK, width), lambda i, _: (i, 0))
    by_col = lambda height: pl.BlockSpec((height, BLOCK), lambda i, _: (0, i))
    return call(
        functools.partial(qkv_kernel, q_heads, kv_heads, len(pieces)),
        (rows // BLOCK,),
        [by_row(D), whole(1, HEAD_SIZE), whole(1, HEAD_SIZE), by_row(HEAD_SIZE), by_row(HEAD_SIZE)]
        + [whole(*piece.shape) for piece in pieces],
        [made(D, w_cols), by_row(q_cols), by_row(k_cols), by_row(2 * k_cols), by_col(k_cols),
         by_row(q_cols), by_row(k_cols)],
        [near_shape((D, w_cols), HALF), near_shape((rows, q_cols), HALF),
         near_shape((rows, k_cols), HALF), near_shape((rows, 2 * k_cols), HALF), far_shape((k_cols, rows), HALF),
         far_shape((rows, q_cols), FULL), far_shape((rows, k_cols), FULL)],
        (h_att, g_query[None], g_key[None], far(cosine), far(sine)) + tuple(far(piece) for piece in pieces),
        table=table,
        flops=2 * rows * D * cols,
        after=after,
    )


def picked(*dims):
    return pl.BlockSpec(dims, lambda i, tab: (tab[i], 0))


def picked_col(*dims):
    return pl.BlockSpec(dims, lambda i, tab: (0, tab[i]))


def stepped(*dims):
    return pl.BlockSpec(dims, lambda i, *_: (i, 0))


def stepped_col(*dims):
    return pl.BlockSpec(dims, lambda i, *_: (0, i))


def halves_of(steps, *dims):
    half = steps // 2
    return [
        pl.BlockSpec(dims, lambda i, *_: (jnp.minimum(i, half - 1), 0)),
        pl.BlockSpec(dims, lambda i, *_: (jnp.maximum(i - half, 0), 0)),
    ]


def half_shapes(rows):
    return [shape_of((rows // 2, D), HALF), shape_of((rows // 2, D), FULL)]


def put_halves(step, steps, part, send_ref, keep_ref):
    @pl.when(step < steps // 2)
    def _():
        send_ref[...] = part.astype(HALF)

    @pl.when(step >= steps // 2)
    def _():
        keep_ref[...] = part


def take_halves(step, steps, theirs, mine, target):
    @pl.when(step < steps // 2)
    def _():
        target[...] = theirs[...]

    @pl.when(step >= steps // 2)
    def _():
        target[...] = mine[...]


def mask_of(seg_keys, seg_queries, key_at, query_at, diagonal, key_axis):
    same = seg_keys == seg_queries
    if not diagonal:
        return same
    key_pos = key_at + lax.broadcasted_iota(jnp.int32, same.shape, key_axis)
    query_pos = query_at + lax.broadcasted_iota(jnp.int32, same.shape, 1 - key_axis)
    return (same & (key_pos < query_pos)) | (key_pos == query_pos)


def over_keys(tab_ref, steps, visit):
    step = pl.program_id(0)
    last = tab_ref[step]
    query_at = last * BLOCK
    visit(pl.multiple_of(query_at, BLOCK), query_at, True)

    def body(key_block, carry):
        visit(pl.multiple_of(key_block * BLOCK, BLOCK), query_at, False)
        return carry

    lax.fori_loop(tab_ref[steps + step], last, body, 0)


def heads_of(index):
    return slice(index * HEAD_SIZE, (index + 1) * HEAD_SIZE)


def attend_kernel(steps, q_heads, group, tab_ref, q_ref, k_ref, v_ref, segq_ref, segk_ref,
                  att_ref, att_t_ref, log_ref, q_scr, out_scr):
    shared_heads = q_heads // group
    high = group * BLOCK
    for head in range(q_heads):
        q_scr[head * BLOCK : (head + 1) * BLOCK, :] = q_ref[:, heads_of(head)]
    out_scr[...] = jnp.zeros(out_scr.shape, FULL)

    def visit(key_at, query_at, diagonal):
        keys = pl.ds(key_at, BLOCK)
        mask = mask_of(segk_ref[:, keys], segq_ref[...], key_at, query_at, diagonal, 1)
        mask = jnp.concatenate([mask] * group, axis=0)
        for shared in range(shared_heads):
            at = slice(shared * high, (shared + 1) * high)
            scores = mul(q_scr[at, :], k_ref[keys, heads_of(shared)], NT)
            expo = jnp.where(mask, jnp.exp2(scores * SCALE_2), 0.0).astype(HALF)
            out_scr[at, :] += mul(expo, v_ref[keys, 2 * shared * HEAD_SIZE : 2 * (shared + 1) * HEAD_SIZE])

    over_keys(tab_ref, steps, visit)
    for head in range(q_heads):
        at = slice(head * BLOCK, (head + 1) * BLOCK)
        total = out_scr[at, HEAD_SIZE:]
        attended = (out_scr[at, :HEAD_SIZE] / total).astype(HALF)
        att_ref[:, heads_of(head)] = attended
        att_t_ref[heads_of(head), :] = attended.T
        log_ref[head : head + 1, :] = jnp.log2(total).T[:1, :]


def attend(chunk, table, queries, keys, values, seg_col, key_row, group, after):
    rows, q_cols = queries.shape
    k_cols = keys.shape[1]
    q_heads = q_cols // HEAD_SIZE
    size = rows // CHUNKS
    steps = size // BLOCK
    extent = size * (chunk + 1)
    return call(
        functools.partial(attend_kernel, steps, q_heads, group),
        (steps,),
        [picked(BLOCK, q_cols), whole(extent, k_cols), whole(extent, 2 * k_cols), picked(BLOCK, 1),
         whole(1, extent)],
        [stepped(BLOCK, q_cols), stepped_col(q_cols, BLOCK), stepped_col(q_heads, BLOCK)],
        [shape_of((size, q_cols), HALF), far_shape((q_cols, size), HALF), shape_of((q_heads, size), FULL)],
        (near(queries), near(keys), near(values), far(seg_col), key_row),
        scratch=[pltpu.VMEM((q_heads * BLOCK, HEAD_SIZE), HALF), pltpu.VMEM((q_heads * BLOCK, 2 * HEAD_SIZE), FULL)],
        table=table,
        flops=6 * size * q_cols * 1024,
        room=8,
        after=after,
    )


def attend_back_kernel(steps, q_heads, group, first, tab_ref, q_ref, k_ref, v_ref, kt_ref, segq_ref, segk_ref,
                       wo_ref, att_ref, log_ref, rq_ref, gq_ref, cos_ref, sin_ref, theirs_ref, mine_ref, *refs):
    if not first:
        dk_in, dv_in, refs = refs[0], refs[1], refs[2:]
    raw_ref, term_ref, dk_ref, dv_ref, branch_scr, q_scr, datt_scr, log_scr, delta_scr, dq_scr = refs
    step = pl.program_id(0)
    shared_heads = q_heads // group
    wide = group * BLOCK

    @pl.when(step == 0)
    def _():
        term_ref[...] = jnp.zeros(term_ref.shape, FULL)
        if first:
            dk_ref[...] = jnp.zeros(dk_ref.shape, FULL)
            dv_ref[...] = jnp.zeros(dv_ref.shape, FULL)
        else:
            dk_ref[...] = dk_in[...]
            dv_ref[...] = dv_in[...]

    take_halves(step, steps, theirs_ref, mine_ref, branch_scr)
    d_att = mul(branch_scr[...], wo_ref[...]).astype(HALF)
    product = (d_att.astype(FULL) * att_ref[...].astype(FULL)).T
    for head in range(q_heads):
        at = slice(head * BLOCK, (head + 1) * BLOCK)
        q_scr[at, :] = q_ref[:, heads_of(head)]
        datt_scr[at, :] = d_att[:, heads_of(head)]
        log_scr[:, at] = log_ref[head : head + 1, :]
        delta_scr[:, at] = jnp.sum(product[heads_of(head), :], axis=0, keepdims=True)
    dq_scr[...] = jnp.zeros(dq_scr.shape, FULL)

    def visit(key_at, query_at, diagonal):
        keys = pl.ds(key_at, BLOCK)
        mask = mask_of(segk_ref[keys, :], segq_ref[...], key_at, query_at, diagonal, 0)
        mask = jnp.concatenate([mask] * group, axis=1)
        for shared in range(shared_heads):
            at = slice(shared * wide, (shared + 1) * wide)
            own = heads_of(shared)
            scores = mul(k_ref[keys, own], q_scr[at, :], NT)
            probs = jnp.where(mask, jnp.exp2(scores * SCALE_2 - log_scr[:, at]), 0.0)
            value_cols = slice(2 * shared * HEAD_SIZE, (2 * shared + 1) * HEAD_SIZE)
            d_probs = mul(v_ref[keys, value_cols], datt_scr[at, :], NT)
            d_scores = (probs * (d_probs - delta_scr[:, at])).astype(HALF)
            dv_ref[keys, own] += mul(probs.astype(HALF), datt_scr[at, :])
            dk_ref[keys, own] += mul(d_scores, q_scr[at, :])
            dq_scr[:, at] += mul(kt_ref[own, keys], d_scores)

    over_keys(tab_ref, steps, visit)
    cosine, sine = cos_ref[...], sin_ref[...]
    gain = gq_ref[...]
    for head in range(q_heads):
        turned = dq_scr[:, head * BLOCK : (head + 1) * BLOCK].T * SCALE
        d_normed = turned * cosine - pltpu.roll(turned, HEAD_SIZE // 2, 1) * sine
        _, unit, factor = rms_parts(rq_ref[:, heads_of(head)], gain)
        term_ref[...] += jnp.sum(d_normed * unit, axis=0, keepdims=True)
        raw_ref[:, heads_of(head)] = norm_back(d_normed, unit, factor, gain).astype(HALF)


def attend_back(chunk, table, queries, keys, values, keys_t, seg_row, key_col, first_b, att, log_total,
                raw_q, g_query, cosine, sine, pieces, later, group, after):
    rows, q_cols = queries.shape
    k_cols = keys.shape[1]
    q_heads = q_cols // HEAD_SIZE
    size = rows // CHUNKS
    steps = size // BLOCK
    extent = size * (chunk + 1)
    return call(
        functools.partial(attend_back_kernel, steps, q_heads, group, not later),
        (steps,),
        [picked(BLOCK, q_cols), whole(extent, k_cols), whole(extent, 2 * k_cols), whole(k_cols, extent),
         picked_col(1, BLOCK), whole(extent, 1), pl.BlockSpec((D, q_cols), lambda *_: (0, 2)),
         stepped(BLOCK, q_cols), stepped_col(q_heads, BLOCK), picked(BLOCK, q_cols), whole(1, HEAD_SIZE),
         picked(BLOCK, HEAD_SIZE), picked(BLOCK, HEAD_SIZE)]
        + halves_of(steps, BLOCK, D)
        + [whole(extent, k_cols)] * len(later),
        [stepped(BLOCK, q_cols), made(1, HEAD_SIZE), made(extent, k_cols), made(extent, k_cols)],
        [shape_of((size, q_cols), HALF), shape_of((1, HEAD_SIZE), FULL),
         shape_of((extent, k_cols), FULL), shape_of((extent, k_cols), FULL)],
        (near(queries), near(keys), near(values), far(keys_t), seg_row, far(key_col), near(first_b), att, log_total,
         far(raw_q), g_query[None], far(cosine), far(sine)) + tuple(pieces) + tuple(later),
        scratch=[pltpu.VMEM((BLOCK, D), HALF), pltpu.VMEM((q_heads * BLOCK, HEAD_SIZE), HALF),
                 pltpu.VMEM((q_heads * BLOCK, HEAD_SIZE), HALF), pltpu.VMEM((1, q_heads * BLOCK), FULL),
                 pltpu.VMEM((1, q_heads * BLOCK), FULL), pltpu.VMEM((HEAD_SIZE, q_heads * BLOCK), FULL)],
        table=table,
        flops=10 * size * q_cols * 1024 + 2 * size * q_cols * D,
        room=10,
        after=after,
    )


def raw_back_kernel(steps, kv_heads, tab_ref, rawq_ref, dk_ref, dv_ref, rk_ref, gk_ref, cos_ref, sin_ref,
                    w_ref, f_ref, raw_ref, thin_ref, term_ref, send_ref, keep_ref):
    step = pl.program_id(0)

    @pl.when(step == 0)
    def _():
        term_ref[...] = jnp.zeros(term_ref.shape, FULL)

    q_cols = rawq_ref.shape[1]
    k_cols = kv_heads * HEAD_SIZE
    cosine, sine = cos_ref[...], sin_ref[...]
    gain = gk_ref[...]
    raw_ref[:, :q_cols] = rawq_ref[...]
    for head in range(kv_heads):
        turned = dk_ref[:, heads_of(head)] * SCALE
        d_normed = turned * cosine - pltpu.roll(turned, HEAD_SIZE // 2, 1) * sine
        _, unit, factor = rms_parts(rk_ref[:, heads_of(head)], gain)
        term_ref[...] += jnp.sum(d_normed * unit, axis=0, keepdims=True)
        raw_ref[:, q_cols + head * HEAD_SIZE : q_cols + (head + 1) * HEAD_SIZE] = norm_back(
            d_normed, unit, factor, gain
        ).astype(HALF)
    raw_ref[:, q_cols + k_cols :] = dv_ref[...].astype(HALF)
    put_halves(step, steps, mul(raw_ref[...], w_ref[...], NT), send_ref, keep_ref)
    both = mul(stacked(f_ref[...], (0, 1)), raw_ref[...], NT)
    thin_ref[...] = both[:RANK] + both[RANK:]


def raw_back(chunk, table, raw_q_back, d_keys, d_values, raw_k, g_key, cosine, sine, first_b, factor_t, after):
    size, q_cols = raw_q_back.shape
    half = size // 2
    k_cols = raw_k.shape[1]
    cols = q_cols + 2 * k_cols
    return call(
        functools.partial(raw_back_kernel, 2, k_cols // HEAD_SIZE),
        (2,),
        [stepped(half, q_cols), picked(half, k_cols), picked(half, k_cols), picked(half, k_cols),
         whole(1, HEAD_SIZE), picked(half, HEAD_SIZE), picked(half, HEAD_SIZE), whole(D, cols), whole(RANK, cols)],
        [pl.BlockSpec((half, cols), lambda i, tab: (tab[i] - chunk * 2, 0)),
         pl.BlockSpec((RANK, half), lambda i, tab: (0, tab[i] - chunk * 2)), made(1, HEAD_SIZE)]
        + halves_of(2, half, D),
        [shape_of((size, cols), HALF), shape_of((RANK, size), FULL), shape_of((1, HEAD_SIZE), FULL)]
        + half_shapes(size),
        (raw_q_back, d_keys, d_values, far(raw_k), g_key[None], far(cosine), far(sine), near(first_b), factor_t),
        table=table,
        flops=2 * size * D * cols,
        after=after,
        room=8,
    )


def mlp_kernel(tab_ref, grad_ref, theirs_ref, mine_ref, w_ref, ht_ref, act_ref, act_t_ref, dgu_ref, h_scr):
    take_halves(pl.program_id(0), 2, theirs_ref, mine_ref, h_scr)
    ff_cols = act_ref.shape[1]
    h_mlp = h_scr[...]
    d_mlp = grad_ref[...].astype(HALF)
    ht_ref[...] = h_mlp.T
    width = tile_of(ff_cols)
    for at in range(0, ff_cols, width):
        gate = mul(h_mlp, w_ref[:, at : at + width])
        up = mul(h_mlp, w_ref[:, ff_cols + at : ff_cols + at + width])
        d_activ = mul(d_mlp, w_ref[:, 2 * ff_cols + at : 2 * ff_cols + at + width])
        sig = jax.nn.sigmoid(gate)
        silu = gate * sig
        activ = (silu * up).astype(HALF)
        act_ref[:, at : at + width] = activ
        act_t_ref[at : at + width, :] = activ.T
        dgu_ref[:, at : at + width] = (d_activ * up * sig * (1.0 + gate * (1.0 - sig))).astype(HALF)
        dgu_ref[:, ff_cols + at : ff_cols + at + width] = (d_activ * silu).astype(HALF)


def feed_forward(table, out_grad, weights, pieces, after):
    half = pieces[0].shape[0]
    size = 2 * half
    w_cols = weights.shape[1]
    ff_cols = w_cols // 3
    return call(
        mlp_kernel,
        (2,),
        [picked(half, D), whole(half, D), whole(half, D), whole(D, w_cols)],
        [stepped_col(D, half), stepped(half, ff_cols), stepped_col(ff_cols, half), stepped(half, 2 * ff_cols)],
        [shape_of((D, size), HALF), shape_of((size, ff_cols), HALF), shape_of((ff_cols, size), HALF),
         shape_of((size, 2 * ff_cols), HALF)],
        (far(out_grad),) + tuple(far(piece) for piece in pieces) + (weights,),
        scratch=[pltpu.VMEM((half, D), HALF)],
        table=table,
        flops=2 * size * D * ff_cols * 3,
        after=after,
        room=12,
    )


def project_kernel(left_ref, right_ref, send_ref, keep_ref):
    put_halves(pl.program_id(0), 2, mul(left_ref[...], right_ref[...], NT), send_ref, keep_ref)


def project(left, weights, at, after, kept=shape_of):
    size, depth = left.shape
    half = size // 2
    return call(
        project_kernel,
        (2,),
        [stepped(half, depth), pl.BlockSpec((D, depth), lambda *_: (0, at))],
        halves_of(2, half, D),
        [shape_of((half, D), HALF), kept((half, D), FULL)],
        (left, weights),
        flops=2 * size * D * depth,
        after=after,
    )


def mid_kernel(tab_ref, x_ref, part_ref, other_ref, g_ref, resid_ref, h_ref):
    resid = x_ref[...] + (part_ref[...].astype(FULL) + other_ref[...].astype(FULL))
    resid_ref[...] = resid
    h_ref[...] = rms_parts(resid, g_ref[...])[0].astype(HALF)


def mid_back_kernel(tab_ref, grad_ref, part_ref, other_ref, g_ref, resid_ref, delta_ref, branch_ref, term_ref):
    d_h = part_ref[...].astype(FULL) + other_ref[...].astype(FULL)
    _, unit, factor = rms_parts(resid_ref[...], 1.0)
    delta = norm_back(d_h, unit, factor, g_ref[...])
    delta_ref[...] = delta
    branch_ref[...] = (grad_ref[...] + delta).astype(HALF)
    add_term(term_ref, d_h * unit)


def in_back_kernel(tab_ref, x_ref, part_ref, other_ref, g_ref, mid_ref, delta_ref, term_ref):
    d_h = part_ref[...].astype(FULL) + other_ref[...].astype(FULL)
    _, unit, factor = rms_parts(x_ref[...], 1.0)
    delta_ref[...] = (mid_ref[...] + norm_back(d_h, unit, factor, g_ref[...])).astype(HALF)
    add_term(term_ref, d_h * unit)


def add_term(term_ref, product):
    @pl.when(pl.program_id(0) == 0)
    def _():
        term_ref[...] = jnp.zeros(term_ref.shape, FULL)

    term_ref[...] += jnp.sum(product, axis=0, keepdims=True)


def norm_rows(kernel, own_half, base, part, other, gain, extra, kinds, with_term, after=()):
    half = part.shape[0]
    steps = half // ROWS
    rows = stepped(ROWS, D)
    return call(
        kernel,
        (steps,),
        [pl.BlockSpec((ROWS, D), lambda i, tab: (tab[0] * steps + i, 0)), rows, rows, whole(1, D)]
        + [rows] * len(extra),
        [rows] * len(kinds) + [made(1, D)] * with_term,
        [near_shape((half, D), dtype) if dtype == FULL else shape_of((half, D), dtype) for dtype in kinds] + [shape_of((1, D), FULL)] * with_term,
        (far(base), part, other, gain[None]) + tuple(near(item) for item in extra),
        table=own_half,
        after=after,
    )


def delta_kernel(a_ref, b_ref, c_ref, d_ref, out_ref):
    first = a_ref[...].astype(FULL) + b_ref[...].astype(FULL)
    out_ref[...] = (first + (c_ref[...].astype(FULL) + d_ref[...].astype(FULL))).astype(HALF)


def layer_delta(terms, after):
    rows = stepped(ROWS, D)
    half = terms[0].shape[0]
    return call(
        delta_kernel, (half // ROWS,), [rows] * 4, [rows], [shape_of((half, D), HALF)], terms, after=after
    )[0]


def stacked(values, order):
    high = values.astype(HALF).astype(FULL)
    low = values - high
    return jnp.concatenate([low if pick else high for pick in order], axis=0).astype(HALF)


def thin(factor, matrix, dims):
    result = mul(stacked(factor, (0, 1)), matrix.astype(HALF), dims)
    return result[:RANK] + result[RANK:]


def outer(left, right):
    return mul(stacked(left, (0, 0, 1, 1)), stacked(right, (0, 1, 0, 1)), TN)


def tile_of(size):
    return 256 if size % 256 == 0 else 128


def grad_kernel(flipped, thinned, lefts, rights, tab_ref, e_ref, f_ref, *refs):
    left_refs, right_refs, refs = refs[:lefts], refs[lefts : lefts + rights], refs[lefts + rights :]
    m_ref, right_scr = refs[0], refs[-1]
    depth = right_scr.shape[0] // rights
    for number, right in enumerate(right_refs):
        right_scr[number * depth : (number + 1) * depth, :] = right[...].astype(HALF)
    depth = right_scr.shape[0] // lefts
    total = e_ref[...]
    for number, left in enumerate(left_refs):
        total = total + mul(left[...], right_scr[number * depth : (number + 1) * depth, :])
    m_ref[...] = total
    p_ref = refs[1]
    if not thinned:
        p_ref[...] = jnp.zeros(p_ref.shape, FULL)
        return
    if flipped:
        p_ref[...] = thin(f_ref[...], total, NN)
    else:
        @pl.when(pl.program_id(0) == 0)
        def _():
            p_ref[...] = jnp.zeros(p_ref.shape, FULL)

        p_ref[...] += thin(f_ref[...], total, NT)


def merge_grad(table, lefts, rights, error, factor_t, flipped, thinned=True, after=()):
    height, width = error.shape
    tile = tile_of(width)
    by_col = lambda rows: pl.BlockSpec((rows, tile), lambda i, _: (0, i))
    rows = lefts[0][2] * len(lefts)
    depth = rows // len(rights)

    def left_spec(place, width):
        return pl.BlockSpec((height, width), lambda i, _: (0, place))

    def right_spec(place, given):
        return pl.BlockSpec((depth, tile), lambda i, tab: (tab[place] if given else place, i))

    p_shape = (RANK, width if flipped else height)
    p_spec = by_col(RANK) if flipped else made(*p_shape)
    if not thinned:
        p_shape = (RANK, 128)
        p_spec = made(*p_shape)
    return call(
        functools.partial(grad_kernel, flipped, thinned, len(lefts), len(rights)),
        (width // tile,),
        [by_col(height), whole(RANK, height) if flipped else by_col(RANK)]
        + [left_spec(place, size) for _, place, size in lefts]
        + [right_spec(place, given) for _, place, given in rights],
        [by_col(height), p_spec],
        [(far_shape if thinned else shape_of)((height, width), FULL), shape_of(p_shape, FULL)],
        (far(error), factor_t)
        + tuple(left[0] for left in lefts)
        + tuple(far(right[0]) if right[2] else right[0] for right in rights),
        scratch=[pltpu.VMEM((rows, tile), HALF)],
        table=table,
        flops=2 * height * width * rows,
        room=8,
        after=after,
    )


def error_kernel(e_ref, f_ref, p_ref):
    p_ref[...] = thin(f_ref[...], e_ref[...], NT)


def error_factor(error, factor_t, after):
    height, width = error.shape
    return call(
        error_kernel,
        (height // BLOCK,),
        [stepped(BLOCK, width), whole(RANK, width)],
        [stepped_col(RANK, BLOCK)],
        [shape_of((RANK, height), FULL)],
        (far(error), factor_t),
        after=after,
    )[0]


def first_kernel(e_ref, h_ref, *refs):
    p_ref = refs[-1]
    total, at = e_ref[...], 0
    for thin_ref in refs[:-1]:
        rows = thin_ref.shape[1]
        both = mul(stacked(thin_ref[...], (0, 1)), h_ref[:, at : at + rows], NT)
        total, at = total + both[:RANK] + both[RANK:], at + rows
    p_ref[...] = total


def first_factor(error_part, h_t, thins):
    return call(
        first_kernel,
        (1,),
        [whole(RANK, D), whole(*h_t.shape)] + [whole(*part.shape) for part in thins],
        [made(RANK, D)],
        [shape_of((RANK, D), FULL)],
        (error_part, h_t) + tuple(thins),
    )[0]


def orthonormal(block):
    rows = lax.broadcasted_iota(jnp.int32, block.shape, 0)
    for row_id in range(RANK):
        row = block[row_id : row_id + 1, :]
        inner = jnp.sum(block * row, axis=1, keepdims=True)
        inverse = lax.rsqrt(inner[row_id : row_id + 1, :] + 1e-12)
        finished = row * inverse
        later = block - (inner * inverse) * finished
        block = jnp.where(rows == row_id, finished, jnp.where(rows > row_id, later, block))
    return block


def second_kernel(flipped, workers, p_ref, m_ref, hat_ref, q_ref):
    step = pl.program_id(0)
    tile = m_ref.shape[0]

    @pl.when(step == 0)
    def _():
        hat_ref[...] = orthonormal(p_ref[...] / workers)
        if not flipped:
            q_ref[...] = jnp.zeros(q_ref.shape, FULL)

    if flipped:
        q_ref[...] = thin(hat_ref[...], m_ref[...], NT)
    else:
        q_ref[...] += thin(hat_ref[:, pl.ds(pl.multiple_of(step * tile, tile), tile)], m_ref[...], NN)


def second_factor(merged, p_sum, flipped, workers, after=()):
    height, width = merged.shape
    tile = tile_of(height)
    q_shape = (RANK, height if flipped else width)
    return call(
        functools.partial(second_kernel, flipped, workers),
        (height // tile,),
        [whole(RANK, D), pl.BlockSpec((tile, width), lambda i: (i, 0))],
        [made(RANK, D), pl.BlockSpec((RANK, tile), lambda i: (0, i)) if flipped else made(*q_shape)],
        [shape_of((RANK, D), FULL), shape_of(q_shape, FULL)],
        (p_sum, merged),
        flops=64 * height * width,
        after=after,
    )


def final_kernel(flipped, m_ref, hat_ref, q_ref, own_ref, moment_ref, weight_ref, err_ref, nw_ref, nm_ref):
    step = pl.program_id(0)
    tile = m_ref.shape[0]
    at = pl.ds(pl.multiple_of(step * tile, tile), tile)
    if flipped:
        err_ref[...] = m_ref[...] - outer(q_ref[:, at], hat_ref[...])
    else:
        err_ref[...] = m_ref[...] - outer(hat_ref[:, at], q_ref[...])

    @pl.when(step == 0)
    def _():
        if flipped:
            approx = outer(q_ref[...], own_ref[...])
        else:
            approx = outer(own_ref[...], q_ref[...])
        moment = MOMENTUM * moment_ref[...] + approx
        nm_ref[...] = moment
        nw_ref[...] = weight_ref[...] - STEP_RATE * moment


def final_update(merged, p_hat, q_new, p_own, moment, weight, flipped, after=()):
    height, width = merged.shape
    tile = tile_of(height)
    by_row = pl.BlockSpec((tile, width), lambda i: (i, 0))
    own, own_out = whole(*weight.shape), made(*weight.shape)
    return call(
        functools.partial(final_kernel, flipped),
        (height // tile,),
        [by_row, whole(*p_hat.shape), whole(*q_new.shape), whole(*p_own.shape), own, own],
        [by_row, own_out, own_out],
        [shape_of(merged.shape, FULL), shape_of(weight.shape, FULL), shape_of(weight.shape, FULL)],
        (merged, p_hat, q_new, p_own, moment, weight),
        flops=64 * height * width,
        after=after,
    )


def spread_kernel(steps, tab_ref, base_ref, theirs_ref, mine_ref, *refs):
    out_ref, step = refs[-1], pl.program_id(0)

    @pl.when(step < steps // 2)
    def _():
        out_ref[...] = base_ref[...] + theirs_ref[...].astype(FULL)

    @pl.when(step >= steps // 2)
    def _():
        out_ref[...] = base_ref[...] + mine_ref[...].astype(FULL)


def spread(table, base, pieces, before, after=()):
    half = pieces[0].shape[0]
    extra = [] if before is None else [far(before)]
    rows = pl.BlockSpec((half, D), lambda i, tab: (tab[i], 0))
    return call(
        functools.partial(spread_kernel, 2),
        (2,),
        [rows, whole(half, D), whole(half, D)] + [pl.BlockSpec(memory_space=pl.ANY)] * len(extra),
        [rows],
        [far_shape(base.shape, FULL)],
        [far(base)] + list(pieces) + extra,
        table=table,
        aliases={4: 0} if extra else None,
        after=after,
    )[0]


def add_kernel(a_ref, b_ref, out_ref):
    out_ref[...] = a_ref[...] + b_ref[...]


def butterfly_step(values, axis, count, span, after=()):
    if span >= count:
        return values
    other = lax.ppermute(values, axis, [(i, i ^ span) for i in range(count)])
    spec = whole(*values.shape)
    return call(
        add_kernel, (1,), [spec, spec], [made(*values.shape)], [shape_of(values.shape, FULL)], (values, other), after=after
    )[0]


def to_core_mate(values, count):
    return lax.ppermute(values, "tensor", [(i, i ^ 1) for i in range(count)])


def chip_kernel(keep_ref, other_ref, out_ref):
    out_ref[...] = (keep_ref[...] + other_ref[...].astype(FULL)).astype(HALF)


def chip_sum(send, keep, count, after=()):
    rows = stepped(BLOCK, D)
    return call(
        chip_kernel, (send.shape[0] // BLOCK,), [rows, rows], [rows], [shape_of(send.shape, HALF)],
        (keep, to_core_mate(send, count)), after=after,
    )[0]


def across_chips(part, count):
    span = 2
    while True:
        other = lax.ppermute(part, "tensor", [(i, i ^ span) for i in range(count)])
        span *= 2
        if span >= count:
            return part, other
        part = (part.astype(FULL) + other.astype(FULL)).astype(HALF)


def pieces_of(own, count):
    return to_core_mate(own, count), own


def local(
    hidden_in,
    seg_ids,
    token_mask,
    out_grad,
    proj_qkv,
    proj_out,
    proj_gate_up,
    proj_down,
    gains,
    moment_qkv,
    moment_out,
    moment_gate_up,
    moment_down,
    error_qkv,
    error_out,
    error_gate_up,
    error_down,
    factor_qkv,
    factor_out,
    factor_gate_up,
    factor_down,
    gain_moment,
):
    parts = lax.axis_size("tensor")
    workers = lax.axis_size("dp")
    rows = hidden_in.shape[0]
    q_heads = QUERY_HEADS // parts
    kv_heads = KEY_VALUE_HEADS // parts
    group = QUERY_HEADS // KEY_VALUE_HEADS
    half = rows // CHUNKS // 2
    order = list(range(CHUNKS))[::-1]
    first_own = jnp.concatenate([proj_qkv, proj_out.T], axis=1).astype(HALF)
    second_own = jnp.concatenate([proj_gate_up, proj_down.T], axis=1).astype(HALF)
    first_pieces, first_steps = ring_gather(first_own, workers)
    shard_places = ring_places(workers, first_own.shape[0])
    g_att = gains[:D]
    g_mlp = gains[D : 2 * D]
    g_query = gains[2 * D : 2 * D + HEAD_SIZE]
    g_key = gains[2 * D + HEAD_SIZE :]
    cosine, sine = rope_tables(rows)

    core = lax.axis_index("tensor") % 2
    seg_row, seg_col = seg_ids, seg_ids[0][:, None]
    key_row = jnp.where(token_mask == 1, seg_ids, -1)
    key_col = key_row[0][:, None]
    starts = jnp.sum(
        (seg_ids[0][None, :] < seg_ids[0][::BLOCK][:, None]).astype(jnp.int32), axis=1
    ) // BLOCK
    tables, half_tables = [], []
    each = half // BLOCK
    for chunk in range(CHUNKS):
        places = [2 * chunk + 1 - core, 2 * chunk + core]
        half_tables.append(jnp.stack(places).astype(jnp.int32))
        numbers = jnp.stack([place * each + i for place in places for i in range(each)]).astype(jnp.int32)
        tables.append(jnp.concatenate([numbers, starts[numbers]]))
    all_halves = jnp.concatenate([half_tables[chunk] for chunk in order])

    own_half = [table[1:] for table in half_tables]

    factors_t = [factor.T for factor in (factor_qkv, factor_out, factor_gate_up, factor_down)]
    h_att = input_norm(hidden_in, g_att)
    first_b, queries, keys, values, keys_t, raw_q, raw_k = make_qkv(
        shard_places, h_att, first_pieces, g_query, g_key, cosine, sine, q_heads, kv_heads, ()
    )
    second_b = lax.all_gather(stage(second_own, first_steps[-2] + (far(cosine), far(sine), far(key_col), shard_places) + tuple(tables)), "dp", axis=0, tiled=True)

    att, att_t, log_total, att_sum, resid, h_pieces = {}, {}, {}, {}, {}, {}
    after, arrived = (), ()
    for chunk in order:
        att[chunk], att_t[chunk], log_total[chunk] = attend(
            chunk, tables[chunk], queries, keys, values, seg_col, key_row, group, after
        )
        if chunk == order[-1]:
            error_part = error_factor(error_qkv[0], factors_t[0], (log_total[chunk],))
            h_t = turned(h_att, (error_part,))
            arrived = arrived + (far(h_t),)
        part = chip_sum(*project(att[chunk], near(first_b), 2, arrived), parts)
        after = (part,)
        att_sum[chunk] = across_chips(part, parts)
        arrived = att_sum[chunk][1:]
        resid[chunk], h_own = norm_rows(
            mid_kernel, own_half[chunk], hidden_in, *att_sum[chunk], g_mlp, (), (FULL, HALF), 0
        )
        h_pieces[chunk] = pieces_of(h_own, parts)

    two = [(chunk, place) for chunk in order for place in (0, 1)]
    size = 2 * half
    h_mlp_t, activ, activ_t, d_gu, mid_sum, mlp_part, mlp_sum = {}, {}, {}, {}, {}, {}, {}
    arrived = ()
    for chunk in order:
        h_mlp_t[chunk], activ[chunk], activ_t[chunk], d_gu[chunk] = feed_forward(
            half_tables[chunk], out_grad, second_b, h_pieces[chunk], after
        )
        if chunk == order[-1]:
            merged_down, p_down = merge_grad(
                all_halves,
                [(activ_t[other], 0, size) for other in order],
                [(out_grad, number, True) for number in range(len(two))],
                error_down[0], factors_t[3], True,
            )
            mlp_part[order[0]] = project(activ[order[0]], second_b, 2, (p_down,))
            arrived = arrived + mlp_part[order[0]][:1]
        part = chip_sum(*project(d_gu[chunk], second_b, 0, arrived), parts)
        after = (part,)
        mid_sum[chunk] = across_chips(part, parts)
        arrived = mid_sum[chunk][1:]

    merged_gu, p_gu = merge_grad(
        all_halves,
        [(h_mlp_t[chunk], 0, size) for chunk in order],
        [(d_gu[chunk], 0, False) for chunk in order],
        error_gate_up[0], factors_t[2], False, after=after,
    )
    after = (p_gu,)
    for chunk in order[1:]:
        mlp_part[chunk] = project(activ[chunk], second_b, 2, after, far_shape)
        after = mlp_part[chunk][:1]
    branch_pieces, mid_delta = {}, {}
    term_mlp = jnp.zeros((1, D), FULL)
    for chunk in order:
        mid_delta[chunk], d_branch, more = norm_rows(
            mid_back_kernel, own_half[chunk], out_grad, *mid_sum[chunk], g_mlp, (resid[chunk],), (FULL, HALF), 1,
            after if chunk == order[-1] else (),
        )
        term_mlp = term_mlp + more
        branch_pieces[chunk] = pieces_of(d_branch, parts)
    after = (d_branch,)
    mlp_sum[order[0]] = across_chips(chip_sum(*mlp_part[order[0]], parts, (p_gu,)), parts)
    d_raw, thins, in_sum = {}, {}, {}
    later = ()
    term_q, term_k = (jnp.zeros((1, HEAD_SIZE), FULL) for _ in range(2))
    deltas = {}
    arrived = ()
    for chunk in order:
        raw_q_back, more_q, d_keys, d_values = attend_back(
            chunk, tables[chunk], queries, keys, values, keys_t, seg_row, key_col, first_b, att[chunk],
            log_total[chunk], raw_q, g_query, cosine, sine, branch_pieces[chunk], later, group, after
        )
        later = (d_keys, d_values)
        if chunk == order[0]:
            deltas[chunk] = layer_delta(att_sum[chunk] + mlp_sum[chunk], later)
            arrived = (deltas[chunk],)
        d_raw[chunk], thins[chunk], more_k, send, keep = raw_back(
            chunk, half_tables[chunk], raw_q_back, d_keys, d_values, raw_k, g_key, cosine, sine, first_b,
            factors_t[0], arrived
        )
        term_q, term_k = term_q + more_q, term_k + more_k
        part = chip_sum(send, keep, parts)
        after = (part,)
        in_sum[chunk] = across_chips(part, parts)
        arrived = in_sum[chunk][1:]
        if chunk == order[0]:
            merged_out, p_out = merge_grad(
                all_halves,
                [(att_t[other], 0, size) for other in order],
                [(branch_pieces[other][place], 0, False) for other, place in two],
                error_out[0], factors_t[1], True, after=after,
            )
            after = (p_out,)

    p_qkv = first_factor(error_part, h_t, [thins[chunk] for chunk in range(CHUNKS)])
    for chunk in order[1:]:
        mlp_sum[chunk] = across_chips(chip_sum(*mlp_part[chunk], parts, after), parts)
    after = after + (p_qkv,)
    term_att = jnp.zeros((1, D), FULL)
    in_delta = {}
    for chunk in order[:-1]:
        in_delta[chunk], more = norm_rows(
            in_back_kernel, own_half[chunk], hidden_in, *in_sum[chunk], g_att, (mid_delta[chunk],), (HALF,), 1, after
        )
        term_att = term_att + more
    p_all = jnp.concatenate([p_down, p_gu, p_out, p_qkv], axis=1)
    p_all = butterfly_step(p_all, "dp", workers, 1, tuple(in_delta.values()))
    merged_qkv, token = merge_grad(
        all_halves,
        [(h_t, chunk, size) for chunk in order],
        [(d_raw[chunk], 0, False) for chunk in order],
        error_qkv[0], factors_t[0], False, False, (p_all,),
    )
    p_all = butterfly_step(p_all, "dp", workers, 2, (token,))
    layer_out = spread(
        half_tables[order[0]], hidden_in, pieces_of(deltas[order[0]], parts), None, (p_all,)
    )
    p_all = butterfly_step(p_all, "dp", workers, 4, (far(layer_out),))
    p_all = butterfly_step(p_all, "dp", workers, 8)
    in_delta[order[-1]], more = norm_rows(
        in_back_kernel, own_half[order[-1]], hidden_in, *in_sum[order[-1]], g_att, (mid_delta[order[-1]],), (HALF,),
        1, (p_all,),
    )
    term_att = term_att + more
    hat_down, q_down = second_factor(merged_down, p_all[:, :D], True, workers)
    hat_gu, q_gu = second_factor(merged_gu, p_all[:, D : 2 * D], False, workers)
    hat_out, q_out = second_factor(merged_out, p_all[:, 2 * D : 3 * D], True, workers)
    hat_qkv, q_qkv = second_factor(merged_qkv, p_all[:, 3 * D :], False, workers)
    share = 2.0 / parts
    gain_terms = jnp.concatenate(
        [term_att[0] * share, term_mlp[0] * share, term_q[0], term_k[0]]
    ).reshape(RANK, -1)
    q_all = jnp.concatenate([q_down, q_gu, q_out, q_qkv, gain_terms], axis=1)
    cuts = [0]
    for part in (q_down, q_gu, q_out, q_qkv, gain_terms):
        cuts.append(cuts[-1] + part.shape[1])
    after = (q_down, q_gu, q_out, q_qkv)
    input_grad = spread(
        half_tables[order[0]], out_grad, pieces_of(in_delta[order[0]], parts), None, after
    )
    q_all = butterfly_step(q_all, "dp", workers, 1, (far(input_grad),))
    for chunk in order[1:]:
        input_grad = spread(
            half_tables[chunk], out_grad, pieces_of(in_delta[chunk], parts), input_grad, (q_all,)
        )
        deltas[chunk] = layer_delta(att_sum[chunk] + mlp_sum[chunk], (far(input_grad),))
    q_all = butterfly_step(q_all, "dp", workers, 2, (far(input_grad),))
    q_all = butterfly_step(q_all, "dp", workers, 4)
    q_all = butterfly_step(q_all, "dp", workers, 8) / workers
    for chunk in order[1:]:
        layer_out = spread(half_tables[chunk], hidden_in, pieces_of(deltas[chunk], parts), layer_out)
    gain_grad = q_all[:, cuts[4] :]
    for span in (1, 2, 4):
        gain_grad = butterfly_step(gain_grad, "tensor", parts, span)
    new_gain_moment = MOMENTUM * gain_moment + gain_grad.reshape(-1)
    new_gains = gains - GAIN_RATE * new_gain_moment

    own_count = D // workers
    results = {}
    for number, (name, merged, p_hat, moment, weight, flipped) in enumerate((
        ("down", merged_down, hat_down, moment_down, proj_down, True),
        ("gu", merged_gu, hat_gu, moment_gate_up, proj_gate_up, False),
        ("out", merged_out, hat_out, moment_out, proj_out, True),
        ("qkv", merged_qkv, hat_qkv, moment_qkv, proj_qkv, False),
    )):
        q_new = q_all[:, cuts[number] : cuts[number + 1]]
        p_own = lax.dynamic_slice_in_dim(p_hat, lax.axis_index("dp") * own_count, own_count, 1)
        new_error, new_weight, new_moment = final_update(
            merged, p_hat, q_new, p_own, moment, weight, flipped
        )
        results[name] = (new_weight, new_moment, new_error[None], q_new.T)
    ordered = [results[name] for name in ("qkv", "out", "gu", "down")]
    return (
        (layer_out, input_grad)
        + tuple(r[0] for r in ordered)
        + tuple(r[1] for r in ordered)
        + tuple(r[2] for r in ordered)
        + tuple(r[3] for r in ordered)
        + (new_gains, new_gain_moment)
    )


def solution(mesh):
    in_specs = (
        P("dp", None),
        P("dp", None),
        P("dp", None),
        P("dp", None),
        P("dp", "tensor"),
        P("tensor", "dp"),
        P("dp", "tensor"),
        P("tensor", "dp"),
        P(),
        P("dp", "tensor"),
        P("tensor", "dp"),
        P("dp", "tensor"),
        P("tensor", "dp"),
        P("dp", None, "tensor"),
        P("dp", "tensor", None),
        P("dp", None, "tensor"),
        P("dp", "tensor", None),
        P("tensor", None),
        P("tensor", None),
        P("tensor", None),
        P("tensor", None),
        P(),
    )
    out_specs = (
        P("dp", None),
        P("dp", None),
        P("dp", "tensor"),
        P("tensor", "dp"),
        P("dp", "tensor"),
        P("tensor", "dp"),
        P("dp", "tensor"),
        P("tensor", "dp"),
        P("dp", "tensor"),
        P("tensor", "dp"),
        P("dp", None, "tensor"),
        P("dp", "tensor", None),
        P("dp", None, "tensor"),
        P("dp", "tensor", None),
        P("tensor", None),
        P("tensor", None),
        P("tensor", None),
        P("tensor", None),
        P(),
        P(),
    )
    return jax.shard_map(local, mesh=mesh, in_specs=in_specs, out_specs=out_specs, check_vma=False)
```

```python
import functools
import math

import jax
import jax.numpy as jnp
from jax import lax
from jax.experimental import pallas as pl
from jax.experimental.pallas import tpu as pltpu
from jax.sharding import PartitionSpec as P

D = 1024
QUERY_HEADS = 16
KEY_VALUE_HEADS = 8
HEAD_SIZE = 128
FF = 3072
RANK = 8


EPSILON = 1e-06
ROPE_THETA = 1000000.0
MOMENTUM = 0.5
STEP_RATE = 0.003
GAIN_RATE = 0.02
CHUNKS = 2
BLOCK = 256
ROWS = 256
SCALE = 1.0 / math.sqrt(HEAD_SIZE)
SCALE_2 = SCALE / math.log(2.0)
MIB = 1024 * 1024

HALF = jnp.bfloat16
FULL = jnp.float32
NN = (((1,), (0,)), ((), ()))
NT = (((1,), (1,)), ((), ()))
TN = (((0,), (0,)), ((), ()))


def mul(left, right, dims=NN):
    return lax.dot_general(left, right, dims, preferred_element_type=FULL)


def shape_of(dims, dtype):
    return jax.ShapeDtypeStruct(dims, dtype)


def far(array):
    return pltpu.with_memory_space_constraint(array, pltpu.HBM)


def near(array):
    return pltpu.with_memory_space_constraint(array, pltpu.VMEM)


def near_shape(dims, dtype):
    return pltpu.VMEM(dims, dtype)


def far_shape(dims, dtype):
    return pltpu.HBM(dims, dtype)


def whole(*dims):
    return pl.BlockSpec(dims, lambda *_: (0,) * len(dims), pipeline_mode=pl.Buffered(1))


def made(*dims):
    return pl.BlockSpec(dims, lambda *_: (0,) * len(dims))


def block_bytes(spec, array):
    if spec.block_shape is None:
        return 0
    size = array.dtype.itemsize
    *lead, height, width = spec.block_shape
    height = -(-height // (32 // size)) * (32 // size)
    count = 2 if spec.pipeline_mode is None else spec.pipeline_mode.buffer_count
    return math.prod(lead) * height * (-(-width // 128) * 128) * size * count


def call(kernel, grid, in_specs, out_specs, out_shape, args, scratch=(), table=None, flops=0, aliases=None, after=(), room=6):
    moved = sum(math.prod(a.shape) * a.dtype.itemsize for a in list(args) + list(out_shape))
    prefetch = () if table is None else (table,)
    first = len(prefetch) + len(args)
    need = sum(block_bytes(*pair) for pair in zip(list(in_specs) + list(out_specs), list(args) + list(out_shape)))
    need += sum(math.prod(item.shape) * jnp.dtype(item.dtype).itemsize for item in scratch) + room * MIB

    def body(*refs):
        kernel(*refs[:first], *refs[first + len(after) :])

    return pl.pallas_call(
        body,
        grid_spec=pltpu.PrefetchScalarGridSpec(
            num_scalar_prefetch=len(prefetch),
            grid=grid,
            in_specs=list(in_specs) + [pl.BlockSpec(memory_space=pl.ANY)] * len(after),
            out_specs=out_specs,
            scratch_shapes=list(scratch),
        ),
        out_shape=out_shape,
        input_output_aliases=aliases or {},
        compiler_params=pltpu.CompilerParams(vmem_limit_bytes=need),
        cost_estimate=pl.CostEstimate(
            flops=int(flops), bytes_accessed=int(moved), transcendentals=0
        ),
    )(*prefetch, *args, *after)


def rms_parts(values, gain_vec):
    factor = lax.rsqrt(jnp.mean(values * values, axis=-1, keepdims=True) + EPSILON)
    normal = values * factor
    return (normal * gain_vec, normal, factor)


def norm_back(grad_in, normal, factor, gain_vec):
    scaled = grad_in * gain_vec
    return factor * (scaled - normal * jnp.mean(scaled * normal, axis=-1, keepdims=True))


def rope_tables(sequence_length):
    position = jnp.arange(sequence_length, dtype=FULL)
    inverse = ROPE_THETA ** (-(jnp.arange(HEAD_SIZE // 2, dtype=FULL) * 2.0 / HEAD_SIZE))
    angles = position[:, None] * inverse[None, :]
    cosine, sine = jnp.cos(angles), jnp.sin(angles)
    return jnp.concatenate([cosine, cosine], 1), jnp.concatenate([-sine, sine], 1)


def ring_of(count):
    return list(range(0, count, 2)) + list(range(1, count, 2))[::-1]


def ring_step(pair, count, cut=None):
    ring = ring_of(count)
    ahead = [(ring[i], ring[(i + 1) % count]) for i in range(count)]
    back = [(target, source) for source, target in ahead]
    from_left, from_right = pair
    if cut is not None:
        from_left, from_right = from_left[:cut], from_right[cut:]
    return lax.ppermute(from_left, "dp", ahead), lax.ppermute(from_right, "dp", back)


def ring_gather(own, count):
    steps, pair = [], (own, own)
    for _ in range(count // 2 - 1):
        pair = ring_step(pair, count)
        steps.append(pair)
    steps.append(ring_step(pair, count, own.shape[0] // 2))
    return [own] + [piece for step in steps for piece in step], steps


def ring_places(count, shard):
    index = lax.axis_index("dp")
    here = jnp.where(index % 2 == 0, index // 2, count - 1 - index // 2)
    shifts = [0]
    for shift in range(1, count // 2):
        shifts += [count - shift, shift]
    shifts = jnp.array(shifts + [count // 2] * 2, jnp.int32)
    at = (here + shifts) % count
    owner = jnp.where(at < count // 2, 2 * at, 2 * (count - 1 - at) + 1)
    late = (jnp.arange(shifts.shape[0]) == shifts.shape[0] - 1).astype(jnp.int32)
    return (owner * shard + late * (shard // 2)).astype(jnp.int32)


def assemble(tab_ref, first, pieces, target):
    for number, piece in enumerate(pieces):
        rows = piece.shape[0]
        target[pl.ds(pl.multiple_of(tab_ref[first + number], rows), rows), :] = piece[...]


def stage_kernel(in_ref, out_ref):
    out_ref[...] = in_ref[...]


def stage(values, after):
    spec = whole(*values.shape)
    return call(stage_kernel, (1,), [spec], [made(*values.shape)], [shape_of(values.shape, values.dtype)], (values,), after=after)[0]


def input_kernel(x_ref, g_ref, h_ref):
    h_ref[...] = rms_parts(x_ref[...], g_ref[...])[0].astype(HALF)


def input_norm(hidden_in, g_att):
    rows = hidden_in.shape[0]
    by_row = pl.BlockSpec((BLOCK, D), lambda i: (i, 0))
    return call(
        input_kernel, (rows // BLOCK,), [by_row, whole(1, D)], [by_row], [shape_of((rows, D), HALF)],
        (far(hidden_in), g_att[None]),
    )[0]


def turn_kernel(h_ref, ht_ref):
    ht_ref[...] = h_ref[...].T


def turned(h_att, after):
    rows = h_att.shape[0]
    return call(
        turn_kernel,
        (rows // BLOCK,),
        [pl.BlockSpec((BLOCK, D), lambda i: (i, 0))],
        [pl.BlockSpec((D, BLOCK), lambda i: (0, i))],
        [far_shape((D, rows), HALF)],
        (h_att,),
        after=after,
    )[0]


def qkv_kernel(q_heads, kv_heads, count, tab_ref, h_ref, gq_ref, gk_ref, cos_ref, sin_ref, *refs):
    pieces, (w_ref, q_ref, k_ref, v_ref, kt_ref, rq_ref, rk_ref) = refs[:count], refs[count:]

    @pl.when(pl.program_id(0) == 0)
    def _():
        assemble(tab_ref, 0, pieces, w_ref)

    h_att = h_ref[...]
    cosine, sine = cos_ref[...], sin_ref[...]
    ones = jnp.ones((h_att.shape[0], HEAD_SIZE), HALF)
    for pair in range((q_heads + 2 * kv_heads) // 2):
        both = mul(h_att, w_ref[:, 2 * pair * HEAD_SIZE : 2 * (pair + 1) * HEAD_SIZE])
        for part in range(2):
            head = 2 * pair + part
            raw = both[:, heads_of(part)]
            if head >= q_heads + kv_heads:
                at = 2 * (head - q_heads - kv_heads) * HEAD_SIZE
                v_ref[:, at : at + HEAD_SIZE] = raw.astype(HALF)
                v_ref[:, at + HEAD_SIZE : at + 2 * HEAD_SIZE] = ones
                continue
            normed = rms_parts(raw, gq_ref[...] if head < q_heads else gk_ref[...])[0]
            rotated = normed * cosine + pltpu.roll(normed, HEAD_SIZE // 2, 1) * sine
            if head < q_heads:
                rq_ref[:, heads_of(head)] = raw
                q_ref[:, heads_of(head)] = rotated.astype(HALF)
            else:
                rk_ref[:, heads_of(head - q_heads)] = raw
                k_ref[:, heads_of(head - q_heads)] = rotated.astype(HALF)
                kt_ref[heads_of(head - q_heads), :] = rotated.T.astype(HALF)


def make_qkv(table, h_att, pieces, g_query, g_key, cosine, sine, q_heads, kv_heads, after):
    rows = h_att.shape[0]
    q_cols, k_cols = q_heads * HEAD_SIZE, kv_heads * HEAD_SIZE
    cols = q_cols + 2 * k_cols
    w_cols = pieces[0].shape[1]
    by_row = lambda width: pl.BlockSpec((BLOCK, width), lambda i, _: (i, 0))
    by_col = lambda height: pl.BlockSpec((height, BLOCK), lambda i, _: (0, i))
    return call(
        functools.partial(qkv_kernel, q_heads, kv_heads, len(pieces)),
        (rows // BLOCK,),
        [by_row(D), whole(1, HEAD_SIZE), whole(1, HEAD_SIZE), by_row(HEAD_SIZE), by_row(HEAD_SIZE)]
        + [whole(*piece.shape) for piece in pieces],
        [made(D, w_cols), by_row(q_cols), by_row(k_cols), by_row(2 * k_cols), by_col(k_cols),
         by_row(q_cols), by_row(k_cols)],
        [near_shape((D, w_cols), HALF), near_shape((rows, q_cols), HALF),
         near_shape((rows, k_cols), HALF), near_shape((rows, 2 * k_cols), HALF), far_shape((k_cols, rows), HALF),
         far_shape((rows, q_cols), FULL), far_shape((rows, k_cols), FULL)],
        (h_att, g_query[None], g_key[None], far(cosine), far(sine)) + tuple(far(piece) for piece in pieces),
        table=table,
        flops=2 * rows * D * cols,
        after=after,
    )


def picked(*dims):
    return pl.BlockSpec(dims, lambda i, tab: (tab[i], 0))


def picked_col(*dims):
    return pl.BlockSpec(dims, lambda i, tab: (0, tab[i]))


def stepped(*dims):
    return pl.BlockSpec(dims, lambda i, *_: (i, 0))


def stepped_col(*dims):
    return pl.BlockSpec(dims, lambda i, *_: (0, i))


def halves_of(steps, *dims):
    half = steps // 2
    return [
        pl.BlockSpec(dims, lambda i, *_: (jnp.minimum(i, half - 1), 0)),
        pl.BlockSpec(dims, lambda i, *_: (jnp.maximum(i - half, 0), 0)),
    ]


def half_shapes(rows):
    return [shape_of((rows // 2, D), HALF), shape_of((rows // 2, D), FULL)]


def put_halves(step, steps, part, send_ref, keep_ref):
    @pl.when(step < steps // 2)
    def _():
        send_ref[...] = part.astype(HALF)

    @pl.when(step >= steps // 2)
    def _():
        keep_ref[...] = part


def take_halves(step, steps, theirs, mine, target):
    @pl.when(step < steps // 2)
    def _():
        target[...] = theirs[...]

    @pl.when(step >= steps // 2)
    def _():
        target[...] = mine[...]


def mask_of(seg_keys, seg_queries, key_at, query_at, diagonal, key_axis):
    same = seg_keys == seg_queries
    if not diagonal:
        return same
    key_pos = key_at + lax.broadcasted_iota(jnp.int32, same.shape, key_axis)
    query_pos = query_at + lax.broadcasted_iota(jnp.int32, same.shape, 1 - key_axis)
    return (same & (key_pos < query_pos)) | (key_pos == query_pos)


def over_keys(tab_ref, steps, visit):
    step = pl.program_id(0)
    last = tab_ref[step]
    query_at = last * BLOCK
    visit(pl.multiple_of(query_at, BLOCK), query_at, True)

    def body(key_block, carry):
        visit(pl.multiple_of(key_block * BLOCK, BLOCK), query_at, False)
        return carry

    lax.fori_loop(tab_ref[steps + step], last, body, 0)


def heads_of(index):
    return slice(index * HEAD_SIZE, (index + 1) * HEAD_SIZE)


def attend_kernel(steps, q_heads, group, tab_ref, q_ref, k_ref, v_ref, segq_ref, segk_ref,
                  att_ref, att_t_ref, log_ref, q_scr, out_scr):
    shared_heads = q_heads // group
    high = group * BLOCK
    for head in range(q_heads):
        q_scr[head * BLOCK : (head + 1) * BLOCK, :] = q_ref[:, heads_of(head)]
    out_scr[...] = jnp.zeros(out_scr.shape, FULL)

    def visit(key_at, query_at, diagonal):
        keys = pl.ds(key_at, BLOCK)
        mask = mask_of(segk_ref[:, keys], segq_ref[...], key_at, query_at, diagonal, 1)
        mask = jnp.concatenate([mask] * group, axis=0)
        for shared in range(shared_heads):
            at = slice(shared * high, (shared + 1) * high)
            scores = mul(q_scr[at, :], k_ref[keys, heads_of(shared)], NT)
            expo = jnp.where(mask, jnp.exp2(scores * SCALE_2), 0.0).astype(HALF)
            out_scr[at, :] += mul(expo, v_ref[keys, 2 * shared * HEAD_SIZE : 2 * (shared + 1) * HEAD_SIZE])

    over_keys(tab_ref, steps, visit)
    for head in range(q_heads):
        at = slice(head * BLOCK, (head + 1) * BLOCK)
        total = out_scr[at, HEAD_SIZE:]
        attended = (out_scr[at, :HEAD_SIZE] / total).astype(HALF)
        att_ref[:, heads_of(head)] = attended
        att_t_ref[heads_of(head), :] = attended.T
        log_ref[head : head + 1, :] = jnp.log2(total).T[:1, :]


def attend(chunk, table, queries, keys, values, seg_col, key_row, group, after):
    rows, q_cols = queries.shape
    k_cols = keys.shape[1]
    q_heads = q_cols // HEAD_SIZE
    size = rows // CHUNKS
    steps = size // BLOCK
    extent = size * (chunk + 1)
    return call(
        functools.partial(attend_kernel, steps, q_heads, group),
        (steps,),
        [picked(BLOCK, q_cols), whole(extent, k_cols), whole(extent, 2 * k_cols), picked(BLOCK, 1),
         whole(1, extent)],
        [stepped(BLOCK, q_cols), stepped_col(q_cols, BLOCK), stepped_col(q_heads, BLOCK)],
        [shape_of((size, q_cols), HALF), far_shape((q_cols, size), HALF), shape_of((q_heads, size), FULL)],
        (near(queries), near(keys), near(values), far(seg_col), key_row),
        scratch=[pltpu.VMEM((q_heads * BLOCK, HEAD_SIZE), HALF), pltpu.VMEM((q_heads * BLOCK, 2 * HEAD_SIZE), FULL)],
        table=table,
        flops=6 * size * q_cols * 1024,
        room=8,
        after=after,
    )


def attend_back_kernel(steps, q_heads, group, first, tab_ref, q_ref, k_ref, v_ref, kt_ref, segq_ref, segk_ref,
                       wo_ref, att_ref, log_ref, rq_ref, gq_ref, cos_ref, sin_ref, theirs_ref, mine_ref, *refs):
    if not first:
        dk_in, dv_in, refs = refs[0], refs[1], refs[2:]
    raw_ref, term_ref, dk_ref, dv_ref, branch_scr, q_scr, datt_scr, log_scr, delta_scr, dq_scr = refs
    step = pl.program_id(0)
    shared_heads = q_heads // group
    wide = group * BLOCK

    @pl.when(step == 0)
    def _():
        term_ref[...] = jnp.zeros(term_ref.shape, FULL)
        if first:
            dk_ref[...] = jnp.zeros(dk_ref.shape, FULL)
            dv_ref[...] = jnp.zeros(dv_ref.shape, FULL)
        else:
            dk_ref[...] = dk_in[...]
            dv_ref[...] = dv_in[...]

    take_halves(step, steps, theirs_ref, mine_ref, branch_scr)
    d_att = mul(branch_scr[...], wo_ref[...]).astype(HALF)
    product = (d_att.astype(FULL) * att_ref[...].astype(FULL)).T
    for head in range(q_heads):
        at = slice(head * BLOCK, (head + 1) * BLOCK)
        q_scr[at, :] = q_ref[:, heads_of(head)]
        datt_scr[at, :] = d_att[:, heads_of(head)]
        log_scr[:, at] = log_ref[head : head + 1, :]
        delta_scr[:, at] = jnp.sum(product[heads_of(head), :], axis=0, keepdims=True)
    dq_scr[...] = jnp.zeros(dq_scr.shape, FULL)

    def visit(key_at, query_at, diagonal):
        keys = pl.ds(key_at, BLOCK)
        mask = mask_of(segk_ref[keys, :], segq_ref[...], key_at, query_at, diagonal, 0)
        mask = jnp.concatenate([mask] * group, axis=1)
        for shared in range(shared_heads):
            at = slice(shared * wide, (shared + 1) * wide)
            own = heads_of(shared)
            scores = mul(k_ref[keys, own], q_scr[at, :], NT)
            probs = jnp.where(mask, jnp.exp2(scores * SCALE_2 - log_scr[:, at]), 0.0)
            value_cols = slice(2 * shared * HEAD_SIZE, (2 * shared + 1) * HEAD_SIZE)
            d_probs = mul(v_ref[keys, value_cols], datt_scr[at, :], NT)
            d_scores = (probs * (d_probs - delta_scr[:, at])).astype(HALF)
            dv_ref[keys, own] += mul(probs.astype(HALF), datt_scr[at, :])
            dk_ref[keys, own] += mul(d_scores, q_scr[at, :])
            dq_scr[:, at] += mul(kt_ref[own, keys], d_scores)

    over_keys(tab_ref, steps, visit)
    cosine, sine = cos_ref[...], sin_ref[...]
    gain = gq_ref[...]
    for head in range(q_heads):
        turned = dq_scr[:, head * BLOCK : (head + 1) * BLOCK].T * SCALE
        d_normed = turned * cosine - pltpu.roll(turned, HEAD_SIZE // 2, 1) * sine
        _, unit, factor = rms_parts(rq_ref[:, heads_of(head)], gain)
        term_ref[...] += jnp.sum(d_normed * unit, axis=0, keepdims=True)
        raw_ref[:, heads_of(head)] = norm_back(d_normed, unit, factor, gain).astype(HALF)


def attend_back(chunk, table, queries, keys, values, keys_t, seg_row, key_col, first_b, att, log_total,
                raw_q, g_query, cosine, sine, pieces, later, group, after):
    rows, q_cols = queries.shape
    k_cols = keys.shape[1]
    q_heads = q_cols // HEAD_SIZE
    size = rows // CHUNKS
    steps = size // BLOCK
    extent = size * (chunk + 1)
    return call(
        functools.partial(attend_back_kernel, steps, q_heads, group, not later),
        (steps,),
        [picked(BLOCK, q_cols), whole(extent, k_cols), whole(extent, 2 * k_cols), whole(k_cols, extent),
         picked_col(1, BLOCK), whole(extent, 1), pl.BlockSpec((D, q_cols), lambda *_: (0, 2)),
         stepped(BLOCK, q_cols), stepped_col(q_heads, BLOCK), picked(BLOCK, q_cols), whole(1, HEAD_SIZE),
         picked(BLOCK, HEAD_SIZE), picked(BLOCK, HEAD_SIZE)]
        + halves_of(steps, BLOCK, D)
        + [whole(extent, k_cols)] * len(later),
        [stepped(BLOCK, q_cols), made(1, HEAD_SIZE), made(extent, k_cols), made(extent, k_cols)],
        [shape_of((size, q_cols), HALF), shape_of((1, HEAD_SIZE), FULL),
         shape_of((extent, k_cols), FULL), shape_of((extent, k_cols), FULL)],
        (near(queries), near(keys), near(values), far(keys_t), seg_row, far(key_col), near(first_b), att, log_total,
         far(raw_q), g_query[None], far(cosine), far(sine)) + tuple(pieces) + tuple(later),
        scratch=[pltpu.VMEM((BLOCK, D), HALF), pltpu.VMEM((q_heads * BLOCK, HEAD_SIZE), HALF),
                 pltpu.VMEM((q_heads * BLOCK, HEAD_SIZE), HALF), pltpu.VMEM((1, q_heads * BLOCK), FULL),
                 pltpu.VMEM((1, q_heads * BLOCK), FULL), pltpu.VMEM((HEAD_SIZE, q_heads * BLOCK), FULL)],
        table=table,
        flops=10 * size * q_cols * 1024 + 2 * size * q_cols * D,
        room=10,
        after=after,
    )


def raw_back_kernel(steps, kv_heads, tab_ref, rawq_ref, dk_ref, dv_ref, rk_ref, gk_ref, cos_ref, sin_ref,
                    w_ref, f_ref, raw_ref, thin_ref, term_ref, send_ref, keep_ref):
    step = pl.program_id(0)

    @pl.when(step == 0)
    def _():
        term_ref[...] = jnp.zeros(term_ref.shape, FULL)

    q_cols = rawq_ref.shape[1]
    k_cols = kv_heads * HEAD_SIZE
    cosine, sine = cos_ref[...], sin_ref[...]
    gain = gk_ref[...]
    raw_ref[:, :q_cols] = rawq_ref[...]
    for head in range(kv_heads):
        turned = dk_ref[:, heads_of(head)] * SCALE
        d_normed = turned * cosine - pltpu.roll(turned, HEAD_SIZE // 2, 1) * sine
        _, unit, factor = rms_parts(rk_ref[:, heads_of(head)], gain)
        term_ref[...] += jnp.sum(d_normed * unit, axis=0, keepdims=True)
        raw_ref[:, q_cols + head * HEAD_SIZE : q_cols + (head + 1) * HEAD_SIZE] = norm_back(
            d_normed, unit, factor, gain
        ).astype(HALF)
    raw_ref[:, q_cols + k_cols :] = dv_ref[...].astype(HALF)
    put_halves(step, steps, mul(raw_ref[...], w_ref[...], NT), send_ref, keep_ref)
    both = mul(stacked(f_ref[...], (0, 1)), raw_ref[...], NT)
    thin_ref[...] = both[:RANK] + both[RANK:]


def raw_back(chunk, table, raw_q_back, d_keys, d_values, raw_k, g_key, cosine, sine, first_b, factor_t, after):
    size, q_cols = raw_q_back.shape
    half = size // 2
    k_cols = raw_k.shape[1]
    cols = q_cols + 2 * k_cols
    return call(
        functools.partial(raw_back_kernel, 2, k_cols // HEAD_SIZE),
        (2,),
        [stepped(half, q_cols), picked(half, k_cols), picked(half, k_cols), picked(half, k_cols),
         whole(1, HEAD_SIZE), picked(half, HEAD_SIZE), picked(half, HEAD_SIZE), whole(D, cols), whole(RANK, cols)],
        [pl.BlockSpec((half, cols), lambda i, tab: (tab[i] - chunk * 2, 0)),
         pl.BlockSpec((RANK, half), lambda i, tab: (0, tab[i] - chunk * 2)), made(1, HEAD_SIZE)]
        + halves_of(2, half, D),
        [shape_of((size, cols), HALF), shape_of((RANK, size), FULL), shape_of((1, HEAD_SIZE), FULL)]
        + half_shapes(size),
        (raw_q_back, d_keys, d_values, far(raw_k), g_key[None], far(cosine), far(sine), near(first_b), factor_t),
        table=table,
        flops=2 * size * D * cols,
        after=after,
        room=8,
    )


def mlp_kernel(tab_ref, grad_ref, theirs_ref, mine_ref, w_ref, ht_ref, dm_ref, act_ref, act_t_ref, dgu_ref, h_scr):
    take_halves(pl.program_id(0), 2, theirs_ref, mine_ref, h_scr)
    ff_cols = act_ref.shape[1]
    h_mlp = h_scr[...]
    d_mlp = grad_ref[...].astype(HALF)
    dm_ref[...] = d_mlp
    ht_ref[...] = h_mlp.T
    width = tile_of(ff_cols)
    for at in range(0, ff_cols, width):
        gate = mul(h_mlp, w_ref[:, at : at + width])
        up = mul(h_mlp, w_ref[:, ff_cols + at : ff_cols + at + width])
        d_activ = mul(d_mlp, w_ref[:, 2 * ff_cols + at : 2 * ff_cols + at + width])
        sig = jax.nn.sigmoid(gate)
        silu = gate * sig
        activ = (silu * up).astype(HALF)
        act_ref[:, at : at + width] = activ
        act_t_ref[at : at + width, :] = activ.T
        dgu_ref[:, at : at + width] = (d_activ * up * sig * (1.0 + gate * (1.0 - sig))).astype(HALF)
        dgu_ref[:, ff_cols + at : ff_cols + at + width] = (d_activ * silu).astype(HALF)


def feed_forward(table, out_grad, weights, pieces, after):
    half = pieces[0].shape[0]
    size = 2 * half
    w_cols = weights.shape[1]
    ff_cols = w_cols // 3
    return call(
        mlp_kernel,
        (2,),
        [picked(half, D), whole(half, D), whole(half, D), whole(D, w_cols)],
        [stepped_col(D, half), stepped(half, D), stepped(half, ff_cols), stepped_col(ff_cols, half),
         stepped(half, 2 * ff_cols)],
        [shape_of((D, size), HALF), shape_of((size, D), HALF), shape_of((size, ff_cols), HALF),
         shape_of((ff_cols, size), HALF),
         shape_of((size, 2 * ff_cols), HALF)],
        (far(out_grad),) + tuple(far(piece) for piece in pieces) + (weights,),
        scratch=[pltpu.VMEM((half, D), HALF)],
        table=table,
        flops=2 * size * D * ff_cols * 3,
        after=after,
        room=12,
    )


def project_kernel(left_ref, right_ref, send_ref, keep_ref):
    put_halves(pl.program_id(0), 2, mul(left_ref[...], right_ref[...], NT), send_ref, keep_ref)


def project(left, weights, at, after, kept=shape_of):
    size, depth = left.shape
    half = size // 2
    return call(
        project_kernel,
        (2,),
        [stepped(half, depth), pl.BlockSpec((D, depth), lambda *_: (0, at))],
        halves_of(2, half, D),
        [shape_of((half, D), HALF), kept((half, D), FULL)],
        (left, weights),
        flops=2 * size * D * depth,
        after=after,
    )


def mid_kernel(tab_ref, x_ref, part_ref, other_ref, g_ref, resid_ref, h_ref):
    resid = x_ref[...] + (part_ref[...].astype(FULL) + other_ref[...].astype(FULL))
    resid_ref[...] = resid
    h_ref[...] = rms_parts(resid, g_ref[...])[0].astype(HALF)


def mid_back_kernel(tab_ref, grad_ref, part_ref, other_ref, g_ref, resid_ref, delta_ref, branch_ref, term_ref):
    d_h = part_ref[...].astype(FULL) + other_ref[...].astype(FULL)
    _, unit, factor = rms_parts(resid_ref[...], 1.0)
    delta = norm_back(d_h, unit, factor, g_ref[...])
    delta_ref[...] = delta
    branch_ref[...] = (grad_ref[...] + delta).astype(HALF)
    add_term(term_ref, d_h * unit)


def in_back_kernel(tab_ref, x_ref, part_ref, other_ref, g_ref, mid_ref, delta_ref, term_ref):
    d_h = part_ref[...].astype(FULL) + other_ref[...].astype(FULL)
    _, unit, factor = rms_parts(x_ref[...], 1.0)
    delta_ref[...] = (mid_ref[...] + norm_back(d_h, unit, factor, g_ref[...])).astype(HALF)
    add_term(term_ref, d_h * unit)


def add_term(term_ref, product):
    @pl.when(pl.program_id(0) == 0)
    def _():
        term_ref[...] = jnp.zeros(term_ref.shape, FULL)

    term_ref[...] += jnp.sum(product, axis=0, keepdims=True)


def norm_rows(kernel, own_half, base, part, other, gain, extra, kinds, with_term, after=()):
    half = part.shape[0]
    steps = half // ROWS
    rows = stepped(ROWS, D)
    return call(
        kernel,
        (steps,),
        [pl.BlockSpec((ROWS, D), lambda i, tab: (tab[0] * steps + i, 0)), rows, rows, whole(1, D)]
        + [rows] * len(extra),
        [rows] * len(kinds) + [made(1, D)] * with_term,
        [near_shape((half, D), dtype) if dtype == FULL else shape_of((half, D), dtype) for dtype in kinds] + [shape_of((1, D), FULL)] * with_term,
        (far(base), part, other, gain[None]) + tuple(near(item) for item in extra),
        table=own_half,
        after=after,
    )


def delta_kernel(a_ref, b_ref, c_ref, d_ref, out_ref):
    first = a_ref[...].astype(FULL) + b_ref[...].astype(FULL)
    out_ref[...] = (first + (c_ref[...].astype(FULL) + d_ref[...].astype(FULL))).astype(HALF)


def layer_delta(terms, after):
    rows = stepped(ROWS, D)
    half = terms[0].shape[0]
    return call(
        delta_kernel, (half // ROWS,), [rows] * 4, [rows], [shape_of((half, D), HALF)], terms, after=after
    )[0]


def stacked(values, order):
    high = values.astype(HALF).astype(FULL)
    low = values - high
    return jnp.concatenate([low if pick else high for pick in order], axis=0).astype(HALF)


def thin(factor, matrix, dims):
    result = mul(stacked(factor, (0, 1)), matrix.astype(HALF), dims)
    return result[:RANK] + result[RANK:]


def outer(left, right):
    return mul(stacked(left, (0, 0, 1, 1)), stacked(right, (0, 1, 0, 1)), TN)


def tile_of(size):
    return 256 if size % 256 == 0 else 128


def grad_kernel(flipped, thinned, lefts, rights, tab_ref, e_ref, f_ref, *refs):
    left_refs, right_refs, refs = refs[:lefts], refs[lefts : lefts + rights], refs[lefts + rights :]
    m_ref, right_scr = refs[0], refs[-1]
    depth = right_scr.shape[0] // rights
    for number, right in enumerate(right_refs):
        right_scr[number * depth : (number + 1) * depth, :] = right[...].astype(HALF)
    depth = right_scr.shape[0] // lefts
    total = e_ref[...]
    for number, left in enumerate(left_refs):
        total = total + mul(left[...], right_scr[number * depth : (number + 1) * depth, :])
    m_ref[...] = total
    p_ref = refs[1]
    if not thinned:
        p_ref[...] = jnp.zeros(p_ref.shape, FULL)
        return
    if flipped:
        p_ref[...] = thin(f_ref[...], total, NN)
    else:
        @pl.when(pl.program_id(0) == 0)
        def _():
            p_ref[...] = jnp.zeros(p_ref.shape, FULL)

        p_ref[...] += thin(f_ref[...], total, NT)


def merge_grad(table, lefts, rights, error, factor_t, flipped, thinned=True, after=()):
    height, width = error.shape
    tile = tile_of(width)
    by_col = lambda rows: pl.BlockSpec((rows, tile), lambda i, _: (0, i))
    rows = lefts[0][2] * len(lefts)
    depth = rows // len(rights)

    def left_spec(place, width):
        return pl.BlockSpec((height, width), lambda i, _: (0, place))

    def right_spec(place, given):
        return pl.BlockSpec((depth, tile), lambda i, tab: (tab[place] if given else place, i))

    p_shape = (RANK, width if flipped else height)
    p_spec = by_col(RANK) if flipped else made(*p_shape)
    if not thinned:
        p_shape = (RANK, 128)
        p_spec = made(*p_shape)
    return call(
        functools.partial(grad_kernel, flipped, thinned, len(lefts), len(rights)),
        (width // tile,),
        [by_col(height), whole(RANK, height) if flipped else by_col(RANK)]
        + [left_spec(place, size) for _, place, size in lefts]
        + [right_spec(place, given) for _, place, given in rights],
        [by_col(height), p_spec],
        [(far_shape if thinned else shape_of)((height, width), FULL), shape_of(p_shape, FULL)],
        (far(error), factor_t)
        + tuple(left[0] for left in lefts)
        + tuple(far(right[0]) if right[2] else right[0] for right in rights),
        scratch=[pltpu.VMEM((rows, tile), HALF)],
        table=table,
        flops=2 * height * width * rows,
        room=8,
        after=after,
    )


def error_kernel(e_ref, f_ref, p_ref):
    p_ref[...] = thin(f_ref[...], e_ref[...], NT)


def error_factor(error, factor_t, after):
    height, width = error.shape
    return call(
        error_kernel,
        (height // BLOCK,),
        [stepped(BLOCK, width), whole(RANK, width)],
        [stepped_col(RANK, BLOCK)],
        [shape_of((RANK, height), FULL)],
        (far(error), factor_t),
        after=after,
    )[0]


def first_kernel(e_ref, h_ref, *refs):
    p_ref = refs[-1]
    total, at = e_ref[...], 0
    for thin_ref in refs[:-1]:
        rows = thin_ref.shape[1]
        both = mul(stacked(thin_ref[...], (0, 1)), h_ref[:, at : at + rows], NT)
        total, at = total + both[:RANK] + both[RANK:], at + rows
    p_ref[...] = total


def first_factor(error_part, h_t, thins):
    return call(
        first_kernel,
        (1,),
        [whole(RANK, D), whole(*h_t.shape)] + [whole(*part.shape) for part in thins],
        [made(RANK, D)],
        [shape_of((RANK, D), FULL)],
        (error_part, h_t) + tuple(thins),
    )[0]


def orthonormal(block):
    rows = lax.broadcasted_iota(jnp.int32, block.shape, 0)
    for row_id in range(RANK):
        row = block[row_id : row_id + 1, :]
        inner = jnp.sum(block * row, axis=1, keepdims=True)
        inverse = lax.rsqrt(inner[row_id : row_id + 1, :] + 1e-12)
        finished = row * inverse
        later = block - (inner * inverse) * finished
        block = jnp.where(rows == row_id, finished, jnp.where(rows > row_id, later, block))
    return block


def second_kernel(flipped, workers, p_ref, m_ref, hat_ref, q_ref):
    step = pl.program_id(0)
    tile = m_ref.shape[0]

    @pl.when(step == 0)
    def _():
        hat_ref[...] = orthonormal(p_ref[...] / workers)
        if not flipped:
            q_ref[...] = jnp.zeros(q_ref.shape, FULL)

    if flipped:
        q_ref[...] = thin(hat_ref[...], m_ref[...], NT)
    else:
        q_ref[...] += thin(hat_ref[:, pl.ds(pl.multiple_of(step * tile, tile), tile)], m_ref[...], NN)


def second_factor(merged, p_sum, flipped, workers, after=()):
    height, width = merged.shape
    tile = tile_of(height)
    q_shape = (RANK, height if flipped else width)
    return call(
        functools.partial(second_kernel, flipped, workers),
        (height // tile,),
        [whole(RANK, D), pl.BlockSpec((tile, width), lambda i: (i, 0))],
        [made(RANK, D), pl.BlockSpec((RANK, tile), lambda i: (0, i)) if flipped else made(*q_shape)],
        [shape_of((RANK, D), FULL), shape_of(q_shape, FULL)],
        (p_sum, merged),
        flops=64 * height * width,
        after=after,
    )


def final_kernel(flipped, m_ref, hat_ref, q_ref, own_ref, moment_ref, weight_ref, err_ref, nw_ref, nm_ref):
    step = pl.program_id(0)
    tile = m_ref.shape[0]
    at = pl.ds(pl.multiple_of(step * tile, tile), tile)
    if flipped:
        err_ref[...] = m_ref[...] - outer(q_ref[:, at], hat_ref[...])
    else:
        err_ref[...] = m_ref[...] - outer(hat_ref[:, at], q_ref[...])

    @pl.when(step == 0)
    def _():
        if flipped:
            approx = outer(q_ref[...], own_ref[...])
        else:
            approx = outer(own_ref[...], q_ref[...])
        moment = MOMENTUM * moment_ref[...] + approx
        nm_ref[...] = moment
        nw_ref[...] = weight_ref[...] - STEP_RATE * moment


def final_update(merged, p_hat, q_new, p_own, moment, weight, flipped, after=()):
    height, width = merged.shape
    tile = tile_of(height)
    by_row = pl.BlockSpec((tile, width), lambda i: (i, 0))
    own, own_out = whole(*weight.shape), made(*weight.shape)
    return call(
        functools.partial(final_kernel, flipped),
        (height // tile,),
        [by_row, whole(*p_hat.shape), whole(*q_new.shape), whole(*p_own.shape), own, own],
        [by_row, own_out, own_out],
        [shape_of(merged.shape, FULL), shape_of(weight.shape, FULL), shape_of(weight.shape, FULL)],
        (merged, p_hat, q_new, p_own, moment, weight),
        flops=64 * height * width,
        after=after,
    )


def spread_kernel(steps, tab_ref, base_ref, theirs_ref, mine_ref, *refs):
    out_ref, step = refs[-1], pl.program_id(0)

    @pl.when(step < steps // 2)
    def _():
        out_ref[...] = base_ref[...] + theirs_ref[...].astype(FULL)

    @pl.when(step >= steps // 2)
    def _():
        out_ref[...] = base_ref[...] + mine_ref[...].astype(FULL)


def spread(table, base, pieces, before, after=()):
    half = pieces[0].shape[0]
    extra = [] if before is None else [far(before)]
    rows = pl.BlockSpec((half, D), lambda i, tab: (tab[i], 0))
    return call(
        functools.partial(spread_kernel, 2),
        (2,),
        [rows, whole(half, D), whole(half, D)] + [pl.BlockSpec(memory_space=pl.ANY)] * len(extra),
        [rows],
        [far_shape(base.shape, FULL)],
        [far(base)] + list(pieces) + extra,
        table=table,
        aliases={4: 0} if extra else None,
        after=after,
    )[0]


def add_kernel(a_ref, b_ref, out_ref):
    out_ref[...] = a_ref[...] + b_ref[...]


def butterfly_step(values, axis, count, span, after=()):
    if span >= count:
        return values
    other = lax.ppermute(values, axis, [(i, i ^ span) for i in range(count)])
    spec = whole(*values.shape)
    return call(
        add_kernel, (1,), [spec, spec], [made(*values.shape)], [shape_of(values.shape, FULL)], (values, other), after=after
    )[0]


def to_core_mate(values, count):
    return lax.ppermute(values, "tensor", [(i, i ^ 1) for i in range(count)])


def chip_kernel(keep_ref, other_ref, out_ref):
    out_ref[...] = (keep_ref[...] + other_ref[...].astype(FULL)).astype(HALF)


def chip_sum(send, keep, count, after=()):
    rows = stepped(BLOCK, D)
    return call(
        chip_kernel, (send.shape[0] // BLOCK,), [rows, rows], [rows], [shape_of(send.shape, HALF)],
        (keep, to_core_mate(send, count)), after=after,
    )[0]


def across_chips(part, count):
    span = 2
    while True:
        other = lax.ppermute(part, "tensor", [(i, i ^ span) for i in range(count)])
        span *= 2
        if span >= count:
            return part, other
        part = (part.astype(FULL) + other.astype(FULL)).astype(HALF)


def pieces_of(own, count):
    return to_core_mate(own, count), own


def local(
    hidden_in,
    seg_ids,
    token_mask,
    out_grad,
    proj_qkv,
    proj_out,
    proj_gate_up,
    proj_down,
    gains,
    moment_qkv,
    moment_out,
    moment_gate_up,
    moment_down,
    error_qkv,
    error_out,
    error_gate_up,
    error_down,
    factor_qkv,
    factor_out,
    factor_gate_up,
    factor_down,
    gain_moment,
):
    parts = lax.axis_size("tensor")
    workers = lax.axis_size("dp")
    rows = hidden_in.shape[0]
    q_heads = QUERY_HEADS // parts
    kv_heads = KEY_VALUE_HEADS // parts
    group = QUERY_HEADS // KEY_VALUE_HEADS
    half = rows // CHUNKS // 2
    order = list(range(CHUNKS))[::-1]
    first_own = jnp.concatenate([proj_qkv, proj_out.T], axis=1).astype(HALF)
    second_own = jnp.concatenate([proj_gate_up, proj_down.T], axis=1).astype(HALF)
    first_pieces, first_steps = ring_gather(first_own, workers)
    shard_places = ring_places(workers, first_own.shape[0])
    g_att = gains[:D]
    g_mlp = gains[D : 2 * D]
    g_query = gains[2 * D : 2 * D + HEAD_SIZE]
    g_key = gains[2 * D + HEAD_SIZE :]
    cosine, sine = rope_tables(rows)

    core = lax.axis_index("tensor") % 2
    seg_row, seg_col = seg_ids, seg_ids[0][:, None]
    key_row = jnp.where(token_mask == 1, seg_ids, -1)
    key_col = key_row[0][:, None]
    starts = jnp.sum(
        (seg_ids[0][None, :] < seg_ids[0][::BLOCK][:, None]).astype(jnp.int32), axis=1
    ) // BLOCK
    tables, half_tables = [], []
    each = half // BLOCK
    for chunk in range(CHUNKS):
        places = [2 * chunk + 1 - core, 2 * chunk + core]
        half_tables.append(jnp.stack(places).astype(jnp.int32))
        numbers = jnp.stack([place * each + i for place in places for i in range(each)]).astype(jnp.int32)
        tables.append(jnp.concatenate([numbers, starts[numbers]]))
    all_halves = jnp.concatenate([half_tables[chunk] for chunk in order])

    own_half = [table[1:] for table in half_tables]

    factors_t = [factor.T for factor in (factor_qkv, factor_out, factor_gate_up, factor_down)]
    h_att = input_norm(hidden_in, g_att)
    first_b, queries, keys, values, keys_t, raw_q, raw_k = make_qkv(
        shard_places, h_att, first_pieces, g_query, g_key, cosine, sine, q_heads, kv_heads, ()
    )
    second_b = lax.all_gather(stage(second_own, first_steps[-2] + (far(cosine), far(sine), far(key_col), shard_places) + tuple(tables)), "dp", axis=0, tiled=True)

    att, att_t, log_total, att_sum = {}, {}, {}, {}
    after, arrived = (), ()
    for chunk in order:
        att[chunk], att_t[chunk], log_total[chunk] = attend(
            chunk, tables[chunk], queries, keys, values, seg_col, key_row, group, after
        )
        if chunk == order[-1]:
            error_part = error_factor(error_qkv[0], factors_t[0], (log_total[chunk],))
            h_t = turned(h_att, (error_part,))
            arrived = arrived + (far(h_t),)
        part = chip_sum(*project(att[chunk], near(first_b), 2, arrived), parts)
        after = (part,)
        att_sum[chunk] = across_chips(part, parts)
        arrived = att_sum[chunk][1:]

    two = [(chunk, place) for chunk in order for place in (0, 1)]
    size = 2 * half
    h_mlp_t, d_mlp, activ, activ_t, d_gu, mid_sum, mlp_part, mlp_sum = {}, {}, {}, {}, {}, {}, {}, {}
    resid, h_pieces = {}, {}
    arrived = ()
    for chunk in order:
        filled = () if chunk == order[0] else mlp_part[order[0]][:1]
        resid[chunk], h_own = norm_rows(
            mid_kernel, own_half[chunk], hidden_in, *att_sum[chunk], g_mlp, (), (FULL, HALF), 0, filled
        )
        h_pieces[chunk] = pieces_of(h_own, parts)
        h_mlp_t[chunk], d_mlp[chunk], activ[chunk], activ_t[chunk], d_gu[chunk] = feed_forward(
            half_tables[chunk], out_grad, second_b, h_pieces[chunk], after
        )
        if chunk == order[-1]:
            merged_down, p_down = merge_grad(
                all_halves,
                [(activ_t[other], 0, size) for other in order],
                [(d_mlp[other], 0, False) for other in order],
                error_down[0], factors_t[3], True,
            )
            arrived = arrived + (p_down,)
        summed = project(d_gu[chunk], second_b, 0, arrived)
        if chunk == order[0]:
            mlp_part[chunk] = project(activ[chunk], second_b, 2, summed[:1], far_shape)
        part = chip_sum(*summed, parts)
        after = (part,)
        mid_sum[chunk] = across_chips(part, parts)
        arrived = mid_sum[chunk][1:]

    merged_gu, p_gu = merge_grad(
        all_halves,
        [(h_mlp_t[chunk], 0, size) for chunk in order],
        [(d_gu[chunk], 0, False) for chunk in order],
        error_gate_up[0], factors_t[2], False, after=after,
    )
    after = (p_gu,)
    for chunk in order[1:]:
        mlp_part[chunk] = project(activ[chunk], second_b, 2, after, far_shape)
        after = mlp_part[chunk][:1]
    branch_pieces, mid_delta = {}, {}
    term_mlp = jnp.zeros((1, D), FULL)
    for chunk in order:
        mid_delta[chunk], d_branch, more = norm_rows(
            mid_back_kernel, own_half[chunk], out_grad, *mid_sum[chunk], g_mlp, (resid[chunk],), (FULL, HALF), 1,
            after if chunk == order[-1] else (),
        )
        term_mlp = term_mlp + more
        branch_pieces[chunk] = pieces_of(d_branch, parts)
    after = (d_branch,)
    mlp_sum[order[0]] = across_chips(chip_sum(*mlp_part[order[0]], parts, (p_gu,)), parts)
    d_raw, thins, in_sum = {}, {}, {}
    later = ()
    term_q, term_k = (jnp.zeros((1, HEAD_SIZE), FULL) for _ in range(2))
    deltas = {}
    arrived = ()
    for chunk in order:
        raw_q_back, more_q, d_keys, d_values = attend_back(
            chunk, tables[chunk], queries, keys, values, keys_t, seg_row, key_col, first_b, att[chunk],
            log_total[chunk], raw_q, g_query, cosine, sine, branch_pieces[chunk], later, group, after
        )
        later = (d_keys, d_values)
        if chunk == order[0]:
            deltas[chunk] = layer_delta(att_sum[chunk] + mlp_sum[chunk], later)
            arrived = (deltas[chunk],)
        d_raw[chunk], thins[chunk], more_k, send, keep = raw_back(
            chunk, half_tables[chunk], raw_q_back, d_keys, d_values, raw_k, g_key, cosine, sine, first_b,
            factors_t[0], arrived
        )
        term_q, term_k = term_q + more_q, term_k + more_k
        part = chip_sum(send, keep, parts)
        after = (part,)
        in_sum[chunk] = across_chips(part, parts)
        arrived = in_sum[chunk][1:]
        if chunk == order[0]:
            merged_out, p_out = merge_grad(
                all_halves,
                [(att_t[other], 0, size) for other in order],
                [(branch_pieces[other][place], 0, False) for other, place in two],
                error_out[0], factors_t[1], True, after=after,
            )
            after = (p_out,)

    p_qkv = first_factor(error_part, h_t, [thins[chunk] for chunk in range(CHUNKS)])
    for chunk in order[1:]:
        mlp_sum[chunk] = across_chips(chip_sum(*mlp_part[chunk], parts, after), parts)
    after = after + (p_qkv,)
    term_att = jnp.zeros((1, D), FULL)
    in_delta = {}
    for chunk in order[:-1]:
        in_delta[chunk], more = norm_rows(
            in_back_kernel, own_half[chunk], hidden_in, *in_sum[chunk], g_att, (mid_delta[chunk],), (HALF,), 1, after
        )
        term_att = term_att + more
    p_all = jnp.concatenate([p_down, p_gu, p_out, p_qkv], axis=1)
    p_all = butterfly_step(p_all, "dp", workers, 1, tuple(in_delta.values()))
    merged_qkv, token = merge_grad(
        all_halves,
        [(h_t, chunk, size) for chunk in order],
        [(d_raw[chunk], 0, False) for chunk in order],
        error_qkv[0], factors_t[0], False, False, (p_all,),
    )
    p_all = butterfly_step(p_all, "dp", workers, 2, (token,))
    layer_out = spread(
        half_tables[order[0]], hidden_in, pieces_of(deltas[order[0]], parts), None, (p_all,)
    )
    p_all = butterfly_step(p_all, "dp", workers, 4, (far(layer_out),))
    p_all = butterfly_step(p_all, "dp", workers, 8)
    in_delta[order[-1]], more = norm_rows(
        in_back_kernel, own_half[order[-1]], hidden_in, *in_sum[order[-1]], g_att, (mid_delta[order[-1]],), (HALF,),
        1, (p_all,),
    )
    term_att = term_att + more
    hat_down, q_down = second_factor(merged_down, p_all[:, :D], True, workers)
    hat_gu, q_gu = second_factor(merged_gu, p_all[:, D : 2 * D], False, workers)
    hat_out, q_out = second_factor(merged_out, p_all[:, 2 * D : 3 * D], True, workers)
    hat_qkv, q_qkv = second_factor(merged_qkv, p_all[:, 3 * D :], False, workers)
    share = 2.0 / parts
    gain_terms = jnp.concatenate(
        [term_att[0] * share, term_mlp[0] * share, term_q[0], term_k[0]]
    ).reshape(RANK, -1)
    q_all = jnp.concatenate([q_down, q_gu, q_out, q_qkv, gain_terms], axis=1)
    cuts = [0]
    for part in (q_down, q_gu, q_out, q_qkv, gain_terms):
        cuts.append(cuts[-1] + part.shape[1])
    after = (q_down, q_gu, q_out, q_qkv)
    input_grad = spread(
        half_tables[order[0]], out_grad, pieces_of(in_delta[order[0]], parts), None, after
    )
    q_all = butterfly_step(q_all, "dp", workers, 1, (far(input_grad),))
    for chunk in order[1:]:
        deltas[chunk] = layer_delta(att_sum[chunk] + mlp_sum[chunk], (q_all,))
    q_all = butterfly_step(q_all, "dp", workers, 2, (deltas[order[-1]],))
    for chunk in order[1:]:
        input_grad = spread(
            half_tables[chunk], out_grad, pieces_of(in_delta[chunk], parts), input_grad, (q_all,)
        )
    q_all = butterfly_step(q_all, "dp", workers, 4, (far(input_grad),))
    q_all = butterfly_step(q_all, "dp", workers, 8) / workers
    for chunk in order[1:]:
        layer_out = spread(half_tables[chunk], hidden_in, pieces_of(deltas[chunk], parts), layer_out)
    gain_grad = q_all[:, cuts[4] :]
    for span in (1, 2, 4):
        gain_grad = butterfly_step(gain_grad, "tensor", parts, span)
    new_gain_moment = MOMENTUM * gain_moment + gain_grad.reshape(-1)
    new_gains = gains - GAIN_RATE * new_gain_moment

    own_count = D // workers
    results = {}
    for number, (name, merged, p_hat, moment, weight, flipped) in enumerate((
        ("down", merged_down, hat_down, moment_down, proj_down, True),
        ("gu", merged_gu, hat_gu, moment_gate_up, proj_gate_up, False),
        ("out", merged_out, hat_out, moment_out, proj_out, True),
        ("qkv", merged_qkv, hat_qkv, moment_qkv, proj_qkv, False),
    )):
        q_new = q_all[:, cuts[number] : cuts[number + 1]]
        p_own = lax.dynamic_slice_in_dim(p_hat, lax.axis_index("dp") * own_count, own_count, 1)
        new_error, new_weight, new_moment = final_update(
            merged, p_hat, q_new, p_own, moment, weight, flipped
        )
        results[name] = (new_weight, new_moment, new_error[None], q_new.T)
    ordered = [results[name] for name in ("qkv", "out", "gu", "down")]
    return (
        (layer_out, input_grad)
        + tuple(r[0] for r in ordered)
        + tuple(r[1] for r in ordered)
        + tuple(r[2] for r in ordered)
        + tuple(r[3] for r in ordered)
        + (new_gains, new_gain_moment)
    )


def solution(mesh):
    in_specs = (
        P("dp", None),
        P("dp", None),
        P("dp", None),
        P("dp", None),
        P("dp", "tensor"),
        P("tensor", "dp"),
        P("dp", "tensor"),
        P("tensor", "dp"),
        P(),
        P("dp", "tensor"),
        P("tensor", "dp"),
        P("dp", "tensor"),
        P("tensor", "dp"),
        P("dp", None, "tensor"),
        P("dp", "tensor", None),
        P("dp", None, "tensor"),
        P("dp", "tensor", None),
        P("tensor", None),
        P("tensor", None),
        P("tensor", None),
        P("tensor", None),
        P(),
    )
    out_specs = (
        P("dp", None),
        P("dp", None),
        P("dp", "tensor"),
        P("tensor", "dp"),
        P("dp", "tensor"),
        P("tensor", "dp"),
        P("dp", "tensor"),
        P("tensor", "dp"),
        P("dp", "tensor"),
        P("tensor", "dp"),
        P("dp", None, "tensor"),
        P("dp", "tensor", None),
        P("dp", None, "tensor"),
        P("dp", "tensor", None),
        P("tensor", None),
        P("tensor", None),
        P("tensor", None),
        P("tensor", None),
        P(),
        P(),
    )
    return jax.shard_map(local, mesh=mesh, in_specs=in_specs, out_specs=out_specs, check_vma=False)
```

```python
import functools
import math

import jax
import jax.numpy as jnp
from jax import lax
from jax.experimental import pallas as pl
from jax.experimental.pallas import tpu as pltpu
from jax.sharding import PartitionSpec as P

D = 1024
QUERY_HEADS = 16
KEY_VALUE_HEADS = 8
HEAD_SIZE = 128
FF = 3072
RANK = 8


EPSILON = 1e-06
ROPE_THETA = 1000000.0
MOMENTUM = 0.5
STEP_RATE = 0.003
GAIN_RATE = 0.02
CHUNKS = 2
BLOCK = 256
ROWS = 256
SCALE = 1.0 / math.sqrt(HEAD_SIZE)
SCALE_2 = SCALE / math.log(2.0)
MIB = 1024 * 1024

HALF = jnp.bfloat16
FULL = jnp.float32
NN = (((1,), (0,)), ((), ()))
NT = (((1,), (1,)), ((), ()))
TN = (((0,), (0,)), ((), ()))


def mul(left, right, dims=NN):
    return lax.dot_general(left, right, dims, preferred_element_type=FULL)


def shape_of(dims, dtype):
    return jax.ShapeDtypeStruct(dims, dtype)


def far(array):
    return pltpu.with_memory_space_constraint(array, pltpu.HBM)


def near(array):
    return pltpu.with_memory_space_constraint(array, pltpu.VMEM)


def near_shape(dims, dtype):
    return pltpu.VMEM(dims, dtype)


def far_shape(dims, dtype):
    return pltpu.HBM(dims, dtype)


def whole(*dims):
    return pl.BlockSpec(dims, lambda *_: (0,) * len(dims), pipeline_mode=pl.Buffered(1))


def made(*dims):
    return pl.BlockSpec(dims, lambda *_: (0,) * len(dims))


def block_bytes(spec, array):
    if spec.block_shape is None:
        return 0
    size = array.dtype.itemsize
    *lead, height, width = spec.block_shape
    height = -(-height // (32 // size)) * (32 // size)
    count = 2 if spec.pipeline_mode is None else spec.pipeline_mode.buffer_count
    return math.prod(lead) * height * (-(-width // 128) * 128) * size * count


def call(kernel, grid, in_specs, out_specs, out_shape, args, scratch=(), table=None, flops=0, aliases=None, after=(), room=6):
    moved = sum(math.prod(a.shape) * a.dtype.itemsize for a in list(args) + list(out_shape))
    prefetch = () if table is None else (table,)
    first = len(prefetch) + len(args)
    need = sum(block_bytes(*pair) for pair in zip(list(in_specs) + list(out_specs), list(args) + list(out_shape)))
    held = [item for item in scratch if item.memory_space == pltpu.VMEM]
    need += sum(math.prod(item.shape) * jnp.dtype(item.dtype).itemsize for item in held) + room * MIB

    def body(*refs):
        kernel(*refs[:first], *refs[first + len(after) :])

    return pl.pallas_call(
        body,
        grid_spec=pltpu.PrefetchScalarGridSpec(
            num_scalar_prefetch=len(prefetch),
            grid=grid,
            in_specs=list(in_specs) + [pl.BlockSpec(memory_space=pl.ANY)] * len(after),
            out_specs=out_specs,
            scratch_shapes=list(scratch),
        ),
        out_shape=out_shape,
        input_output_aliases=aliases or {},
        compiler_params=pltpu.CompilerParams(vmem_limit_bytes=need),
        cost_estimate=pl.CostEstimate(
            flops=int(flops), bytes_accessed=int(moved), transcendentals=0
        ),
    )(*prefetch, *args, *after)


def rms_parts(values, gain_vec):
    factor = lax.rsqrt(jnp.mean(values * values, axis=-1, keepdims=True) + EPSILON)
    normal = values * factor
    return (normal * gain_vec, normal, factor)


def norm_back(grad_in, normal, factor, gain_vec):
    scaled = grad_in * gain_vec
    return factor * (scaled - normal * jnp.mean(scaled * normal, axis=-1, keepdims=True))


def rope_tables(sequence_length):
    position = jnp.arange(sequence_length, dtype=FULL)
    inverse = ROPE_THETA ** (-(jnp.arange(HEAD_SIZE // 2, dtype=FULL) * 2.0 / HEAD_SIZE))
    angles = position[:, None] * inverse[None, :]
    cosine, sine = jnp.cos(angles), jnp.sin(angles)
    return jnp.concatenate([cosine, cosine], 1), jnp.concatenate([-sine, sine], 1)


def ring_of(count):
    return list(range(0, count, 2)) + list(range(1, count, 2))[::-1]


def ring_step(pair, count, cut=None):
    ring = ring_of(count)
    ahead = [(ring[i], ring[(i + 1) % count]) for i in range(count)]
    back = [(target, source) for source, target in ahead]
    from_left, from_right = pair
    if cut is not None:
        from_left, from_right = from_left[:cut], from_right[cut:]
    return lax.ppermute(from_left, "dp", ahead), lax.ppermute(from_right, "dp", back)


def ring_gather(own, count):
    steps, pair = [], (own, own)
    for _ in range(count // 2 - 1):
        pair = ring_step(pair, count)
        steps.append(pair)
    steps.append(ring_step(pair, count, own.shape[0] // 2))
    return [own] + [piece for step in steps for piece in step], steps


def ring_places(count, shard):
    index = lax.axis_index("dp")
    here = jnp.where(index % 2 == 0, index // 2, count - 1 - index // 2)
    shifts = [0]
    for shift in range(1, count // 2):
        shifts += [count - shift, shift]
    shifts = jnp.array(shifts + [count // 2] * 2, jnp.int32)
    at = (here + shifts) % count
    owner = jnp.where(at < count // 2, 2 * at, 2 * (count - 1 - at) + 1)
    late = (jnp.arange(shifts.shape[0]) == shifts.shape[0] - 1).astype(jnp.int32)
    return (owner * shard + late * (shard // 2)).astype(jnp.int32)


def assemble(tab_ref, first, pieces, target):
    for number, piece in enumerate(pieces):
        rows = piece.shape[0]
        target[pl.ds(pl.multiple_of(tab_ref[first + number], rows), rows), :] = piece[...]


def stage_kernel(in_ref, out_ref):
    out_ref[...] = in_ref[...]


def stage(values, after):
    spec = whole(*values.shape)
    return call(stage_kernel, (1,), [spec], [made(*values.shape)], [shape_of(values.shape, values.dtype)], (values,), after=after)[0]


def input_kernel(x_ref, g_ref, h_ref):
    h_ref[...] = rms_parts(x_ref[...], g_ref[...])[0].astype(HALF)


def input_norm(hidden_in, g_att):
    rows = hidden_in.shape[0]
    by_row = pl.BlockSpec((BLOCK, D), lambda i: (i, 0))
    return call(
        input_kernel, (rows // BLOCK,), [by_row, whole(1, D)], [by_row], [shape_of((rows, D), HALF)],
        (far(hidden_in), g_att[None]),
    )[0]


def turn_kernel(h_ref, ht_ref):
    ht_ref[...] = h_ref[...].T


def turned(h_att, after):
    rows = h_att.shape[0]
    return call(
        turn_kernel,
        (rows // BLOCK,),
        [pl.BlockSpec((BLOCK, D), lambda i: (i, 0))],
        [pl.BlockSpec((D, BLOCK), lambda i: (0, i))],
        [far_shape((D, rows), HALF)],
        (h_att,),
        after=after,
    )[0]


def qkv_kernel(q_heads, kv_heads, count, tab_ref, h_ref, gq_ref, gk_ref, cos_ref, sin_ref, *refs):
    pieces, (w_ref, q_ref, k_ref, v_ref, kt_ref, rq_ref, rk_ref) = refs[:count], refs[count:]

    @pl.when(pl.program_id(0) == 0)
    def _():
        assemble(tab_ref, 0, pieces, w_ref)

    h_att = h_ref[...]
    cosine, sine = cos_ref[...], sin_ref[...]
    ones = jnp.ones((h_att.shape[0], HEAD_SIZE), HALF)
    for pair in range((q_heads + 2 * kv_heads) // 2):
        both = mul(h_att, w_ref[:, 2 * pair * HEAD_SIZE : 2 * (pair + 1) * HEAD_SIZE])
        for part in range(2):
            head = 2 * pair + part
            raw = both[:, heads_of(part)]
            if head >= q_heads + kv_heads:
                at = 2 * (head - q_heads - kv_heads) * HEAD_SIZE
                v_ref[:, at : at + HEAD_SIZE] = raw.astype(HALF)
                v_ref[:, at + HEAD_SIZE : at + 2 * HEAD_SIZE] = ones
                continue
            normed = rms_parts(raw, gq_ref[...] if head < q_heads else gk_ref[...])[0]
            rotated = normed * cosine + pltpu.roll(normed, HEAD_SIZE // 2, 1) * sine
            if head < q_heads:
                rq_ref[:, heads_of(head)] = raw
                q_ref[:, heads_of(head)] = rotated.astype(HALF)
            else:
                rk_ref[:, heads_of(head - q_heads)] = raw
                k_ref[:, heads_of(head - q_heads)] = rotated.astype(HALF)
                kt_ref[heads_of(head - q_heads), :] = rotated.T.astype(HALF)


def make_qkv(table, h_att, pieces, g_query, g_key, cosine, sine, q_heads, kv_heads, after):
    rows = h_att.shape[0]
    q_cols, k_cols = q_heads * HEAD_SIZE, kv_heads * HEAD_SIZE
    cols = q_cols + 2 * k_cols
    w_cols = pieces[0].shape[1]
    by_row = lambda width: pl.BlockSpec((BLOCK, width), lambda i, _: (i, 0))
    by_col = lambda height: pl.BlockSpec((height, BLOCK), lambda i, _: (0, i))
    return call(
        functools.partial(qkv_kernel, q_heads, kv_heads, len(pieces)),
        (rows // BLOCK,),
        [by_row(D), whole(1, HEAD_SIZE), whole(1, HEAD_SIZE), by_row(HEAD_SIZE), by_row(HEAD_SIZE)]
        + [whole(*piece.shape) for piece in pieces],
        [made(D, w_cols), by_row(q_cols), by_row(k_cols), by_row(2 * k_cols), by_col(k_cols),
         by_row(q_cols), by_row(k_cols)],
        [near_shape((D, w_cols), HALF), near_shape((rows, q_cols), HALF),
         near_shape((rows, k_cols), HALF), near_shape((rows, 2 * k_cols), HALF), far_shape((k_cols, rows), HALF),
         far_shape((rows, q_cols), FULL), far_shape((rows, k_cols), FULL)],
        (h_att, g_query[None], g_key[None], far(cosine), far(sine)) + tuple(far(piece) for piece in pieces),
        table=table,
        flops=2 * rows * D * cols,
        after=after,
    )


def picked(*dims):
    return pl.BlockSpec(dims, lambda i, tab: (tab[i], 0))


def picked_col(*dims):
    return pl.BlockSpec(dims, lambda i, tab: (0, tab[i]))


def stepped(*dims):
    return pl.BlockSpec(dims, lambda i, *_: (i, 0))


def stepped_col(*dims):
    return pl.BlockSpec(dims, lambda i, *_: (0, i))


def halves_of(steps, *dims):
    half = steps // 2
    return [
        pl.BlockSpec(dims, lambda i, *_: (jnp.minimum(i, half - 1), 0)),
        pl.BlockSpec(dims, lambda i, *_: (jnp.maximum(i - half, 0), 0)),
    ]


def half_shapes(rows):
    return [shape_of((rows // 2, D), HALF), shape_of((rows // 2, D), FULL)]


def put_halves(step, steps, part, send_ref, keep_ref):
    @pl.when(step < steps // 2)
    def _():
        send_ref[...] = part.astype(HALF)

    @pl.when(step >= steps // 2)
    def _():
        keep_ref[...] = part


def take_halves(step, steps, theirs, mine, target):
    @pl.when(step < steps // 2)
    def _():
        target[...] = theirs[...]

    @pl.when(step >= steps // 2)
    def _():
        target[...] = mine[...]


def mask_of(seg_keys, seg_queries, key_at, query_at, diagonal, key_axis):
    same = seg_keys == seg_queries
    if not diagonal:
        return same
    key_pos = key_at + lax.broadcasted_iota(jnp.int32, same.shape, key_axis)
    query_pos = query_at + lax.broadcasted_iota(jnp.int32, same.shape, 1 - key_axis)
    return (same & (key_pos < query_pos)) | (key_pos == query_pos)


def over_keys(tab_ref, steps, visit):
    step = pl.program_id(0)
    last = tab_ref[step]
    query_at = last * BLOCK
    visit(pl.multiple_of(query_at, BLOCK), query_at, True)

    def body(key_block, carry):
        visit(pl.multiple_of(key_block * BLOCK, BLOCK), query_at, False)
        return carry

    lax.fori_loop(tab_ref[steps + step], last, body, 0)


def heads_of(index):
    return slice(index * HEAD_SIZE, (index + 1) * HEAD_SIZE)


def attend_kernel(steps, q_heads, group, tab_ref, q_ref, k_ref, v_ref, segq_ref, segk_ref,
                  att_ref, att_t_ref, log_ref, q_scr, out_scr):
    shared_heads = q_heads // group
    high = group * BLOCK
    for head in range(q_heads):
        q_scr[head * BLOCK : (head + 1) * BLOCK, :] = q_ref[:, heads_of(head)]
    out_scr[...] = jnp.zeros(out_scr.shape, FULL)

    def visit(key_at, query_at, diagonal):
        keys = pl.ds(key_at, BLOCK)
        mask = mask_of(segk_ref[:, keys], segq_ref[...], key_at, query_at, diagonal, 1)
        mask = jnp.concatenate([mask] * group, axis=0)
        for shared in range(shared_heads):
            at = slice(shared * high, (shared + 1) * high)
            scores = mul(q_scr[at, :], k_ref[keys, heads_of(shared)], NT)
            expo = jnp.where(mask, jnp.exp2(scores * SCALE_2), 0.0).astype(HALF)
            out_scr[at, :] += mul(expo, v_ref[keys, 2 * shared * HEAD_SIZE : 2 * (shared + 1) * HEAD_SIZE])

    over_keys(tab_ref, steps, visit)
    for head in range(q_heads):
        at = slice(head * BLOCK, (head + 1) * BLOCK)
        total = out_scr[at, HEAD_SIZE:]
        attended = (out_scr[at, :HEAD_SIZE] / total).astype(HALF)
        att_ref[:, heads_of(head)] = attended
        att_t_ref[heads_of(head), :] = attended.T
        log_ref[head : head + 1, :] = jnp.log2(total).T[:1, :]


def attend(chunk, table, queries, keys, values, seg_col, key_row, group, after):
    rows, q_cols = queries.shape
    k_cols = keys.shape[1]
    q_heads = q_cols // HEAD_SIZE
    size = rows // CHUNKS
    steps = size // BLOCK
    extent = size * (chunk + 1)
    return call(
        functools.partial(attend_kernel, steps, q_heads, group),
        (steps,),
        [picked(BLOCK, q_cols), whole(extent, k_cols), whole(extent, 2 * k_cols), picked(BLOCK, 1),
         whole(1, extent)],
        [stepped(BLOCK, q_cols), stepped_col(q_cols, BLOCK), stepped_col(q_heads, BLOCK)],
        [shape_of((size, q_cols), HALF), far_shape((q_cols, size), HALF), shape_of((q_heads, size), FULL)],
        (near(queries), near(keys), near(values), far(seg_col), key_row),
        scratch=[pltpu.VMEM((q_heads * BLOCK, HEAD_SIZE), HALF), pltpu.VMEM((q_heads * BLOCK, 2 * HEAD_SIZE), FULL)],
        table=table,
        flops=6 * size * q_cols * 1024,
        room=8,
        after=after,
    )


def attend_back_kernel(steps, q_heads, group, first, tab_ref, q_ref, k_ref, v_ref, kt_ref, segq_ref, segk_ref,
                       wo_ref, att_ref, log_ref, rq_ref, gq_ref, cos_ref, sin_ref, theirs_ref, mine_ref, *refs):
    if not first:
        dk_in, dv_in, refs = refs[0], refs[1], refs[2:]
    raw_ref, term_ref, dk_ref, dv_ref, branch_scr, q_scr, datt_scr, log_scr, delta_scr, dq_scr = refs
    step = pl.program_id(0)
    shared_heads = q_heads // group
    wide = group * BLOCK

    @pl.when(step == 0)
    def _():
        term_ref[...] = jnp.zeros(term_ref.shape, FULL)
        if first:
            dk_ref[...] = jnp.zeros(dk_ref.shape, FULL)
            dv_ref[...] = jnp.zeros(dv_ref.shape, FULL)
        else:
            dk_ref[...] = dk_in[...]
            dv_ref[...] = dv_in[...]

    take_halves(step, steps, theirs_ref, mine_ref, branch_scr)
    d_att = mul(branch_scr[...], wo_ref[...]).astype(HALF)
    product = (d_att.astype(FULL) * att_ref[...].astype(FULL)).T
    for head in range(q_heads):
        at = slice(head * BLOCK, (head + 1) * BLOCK)
        q_scr[at, :] = q_ref[:, heads_of(head)]
        datt_scr[at, :] = d_att[:, heads_of(head)]
        log_scr[:, at] = log_ref[head : head + 1, :]
        delta_scr[:, at] = jnp.sum(product[heads_of(head), :], axis=0, keepdims=True)
    dq_scr[...] = jnp.zeros(dq_scr.shape, FULL)

    def visit(key_at, query_at, diagonal):
        keys = pl.ds(key_at, BLOCK)
        mask = mask_of(segk_ref[keys, :], segq_ref[...], key_at, query_at, diagonal, 0)
        mask = jnp.concatenate([mask] * group, axis=1)
        for shared in range(shared_heads):
            at = slice(shared * wide, (shared + 1) * wide)
            own = heads_of(shared)
            scores = mul(k_ref[keys, own], q_scr[at, :], NT)
            probs = jnp.where(mask, jnp.exp2(scores * SCALE_2 - log_scr[:, at]), 0.0)
            value_cols = slice(2 * shared * HEAD_SIZE, (2 * shared + 1) * HEAD_SIZE)
            d_probs = mul(v_ref[keys, value_cols], datt_scr[at, :], NT)
            d_scores = (probs * (d_probs - delta_scr[:, at])).astype(HALF)
            dv_ref[keys, own] += mul(probs.astype(HALF), datt_scr[at, :])
            dk_ref[keys, own] += mul(d_scores, q_scr[at, :])
            dq_scr[:, at] += mul(kt_ref[own, keys], d_scores)

    over_keys(tab_ref, steps, visit)
    cosine, sine = cos_ref[...], sin_ref[...]
    gain = gq_ref[...]
    for head in range(q_heads):
        turned = dq_scr[:, head * BLOCK : (head + 1) * BLOCK].T * SCALE
        d_normed = turned * cosine - pltpu.roll(turned, HEAD_SIZE // 2, 1) * sine
        _, unit, factor = rms_parts(rq_ref[:, heads_of(head)], gain)
        term_ref[...] += jnp.sum(d_normed * unit, axis=0, keepdims=True)
        raw_ref[:, heads_of(head)] = norm_back(d_normed, unit, factor, gain).astype(HALF)


def attend_back(chunk, table, queries, keys, values, keys_t, seg_row, key_col, first_b, att, log_total,
                raw_q, g_query, cosine, sine, pieces, later, group, after):
    rows, q_cols = queries.shape
    k_cols = keys.shape[1]
    q_heads = q_cols // HEAD_SIZE
    size = rows // CHUNKS
    steps = size // BLOCK
    extent = size * (chunk + 1)
    return call(
        functools.partial(attend_back_kernel, steps, q_heads, group, not later),
        (steps,),
        [picked(BLOCK, q_cols), whole(extent, k_cols), whole(extent, 2 * k_cols), whole(k_cols, extent),
         picked_col(1, BLOCK), whole(extent, 1), pl.BlockSpec((D, q_cols), lambda *_: (0, 2)),
         stepped(BLOCK, q_cols), stepped_col(q_heads, BLOCK), picked(BLOCK, q_cols), whole(1, HEAD_SIZE),
         picked(BLOCK, HEAD_SIZE), picked(BLOCK, HEAD_SIZE)]
        + halves_of(steps, BLOCK, D)
        + [whole(extent, k_cols)] * len(later),
        [stepped(BLOCK, q_cols), made(1, HEAD_SIZE), made(extent, k_cols), made(extent, k_cols)],
        [shape_of((size, q_cols), HALF), shape_of((1, HEAD_SIZE), FULL),
         shape_of((extent, k_cols), FULL), shape_of((extent, k_cols), FULL)],
        (near(queries), near(keys), near(values), far(keys_t), seg_row, far(key_col), near(first_b), att, log_total,
         far(raw_q), g_query[None], far(cosine), far(sine)) + tuple(pieces) + tuple(later),
        scratch=[pltpu.VMEM((BLOCK, D), HALF), pltpu.VMEM((q_heads * BLOCK, HEAD_SIZE), HALF),
                 pltpu.VMEM((q_heads * BLOCK, HEAD_SIZE), HALF), pltpu.VMEM((1, q_heads * BLOCK), FULL),
                 pltpu.VMEM((1, q_heads * BLOCK), FULL), pltpu.VMEM((HEAD_SIZE, q_heads * BLOCK), FULL)],
        table=table,
        flops=10 * size * q_cols * 1024 + 2 * size * q_cols * D,
        room=10,
        after=after,
    )


def raw_back_kernel(steps, kv_heads, tab_ref, rawq_ref, dk_ref, dv_ref, rk_ref, gk_ref, cos_ref, sin_ref,
                    w_ref, f_ref, raw_ref, thin_ref, term_ref, send_ref, keep_ref):
    step = pl.program_id(0)

    @pl.when(step == 0)
    def _():
        term_ref[...] = jnp.zeros(term_ref.shape, FULL)

    q_cols = rawq_ref.shape[1]
    k_cols = kv_heads * HEAD_SIZE
    cosine, sine = cos_ref[...], sin_ref[...]
    gain = gk_ref[...]
    raw_ref[:, :q_cols] = rawq_ref[...]
    for head in range(kv_heads):
        turned = dk_ref[:, heads_of(head)] * SCALE
        d_normed = turned * cosine - pltpu.roll(turned, HEAD_SIZE // 2, 1) * sine
        _, unit, factor = rms_parts(rk_ref[:, heads_of(head)], gain)
        term_ref[...] += jnp.sum(d_normed * unit, axis=0, keepdims=True)
        raw_ref[:, q_cols + head * HEAD_SIZE : q_cols + (head + 1) * HEAD_SIZE] = norm_back(
            d_normed, unit, factor, gain
        ).astype(HALF)
    raw_ref[:, q_cols + k_cols :] = dv_ref[...].astype(HALF)
    put_halves(step, steps, mul(raw_ref[...], w_ref[...], NT), send_ref, keep_ref)
    both = mul(stacked(f_ref[...], (0, 1)), raw_ref[...], NT)
    thin_ref[...] = both[:RANK] + both[RANK:]


def raw_back(chunk, table, raw_q_back, d_keys, d_values, raw_k, g_key, cosine, sine, first_b, factor_t, after):
    size, q_cols = raw_q_back.shape
    half = size // 2
    k_cols = raw_k.shape[1]
    cols = q_cols + 2 * k_cols
    return call(
        functools.partial(raw_back_kernel, 2, k_cols // HEAD_SIZE),
        (2,),
        [stepped(half, q_cols), picked(half, k_cols), picked(half, k_cols), picked(half, k_cols),
         whole(1, HEAD_SIZE), picked(half, HEAD_SIZE), picked(half, HEAD_SIZE), whole(D, cols), whole(RANK, cols)],
        [pl.BlockSpec((half, cols), lambda i, tab: (tab[i] - chunk * 2, 0)),
         pl.BlockSpec((RANK, half), lambda i, tab: (0, tab[i] - chunk * 2)), made(1, HEAD_SIZE)]
        + halves_of(2, half, D),
        [shape_of((size, cols), HALF), shape_of((RANK, size), FULL), shape_of((1, HEAD_SIZE), FULL)]
        + half_shapes(size),
        (raw_q_back, d_keys, d_values, far(raw_k), g_key[None], far(cosine), far(sine), near(first_b), factor_t),
        table=table,
        flops=2 * size * D * cols,
        after=after,
        room=8,
    )


def mlp_kernel(tab_ref, grad_ref, theirs_ref, mine_ref, w_ref, ht_ref, dm_ref, act_ref, act_t_ref, dgu_ref, h_scr):
    take_halves(pl.program_id(0), 2, theirs_ref, mine_ref, h_scr)
    ff_cols = act_ref.shape[1]
    h_mlp = h_scr[...]
    d_mlp = grad_ref[...].astype(HALF)
    dm_ref[...] = d_mlp
    ht_ref[...] = h_mlp.T
    width = tile_of(ff_cols)
    for at in range(0, ff_cols, width):
        gate = mul(h_mlp, w_ref[:, at : at + width])
        up = mul(h_mlp, w_ref[:, ff_cols + at : ff_cols + at + width])
        d_activ = mul(d_mlp, w_ref[:, 2 * ff_cols + at : 2 * ff_cols + at + width])
        sig = jax.nn.sigmoid(gate)
        silu = gate * sig
        activ = (silu * up).astype(HALF)
        act_ref[:, at : at + width] = activ
        act_t_ref[at : at + width, :] = activ.T
        dgu_ref[:, at : at + width] = (d_activ * up * sig * (1.0 + gate * (1.0 - sig))).astype(HALF)
        dgu_ref[:, ff_cols + at : ff_cols + at + width] = (d_activ * silu).astype(HALF)


def feed_forward(table, out_grad, weights, pieces, after):
    half = pieces[0].shape[0]
    size = 2 * half
    w_cols = weights.shape[1]
    ff_cols = w_cols // 3
    return call(
        mlp_kernel,
        (2,),
        [picked(half, D), whole(half, D), whole(half, D), whole(D, w_cols)],
        [stepped_col(D, half), stepped(half, D), stepped(half, ff_cols), stepped_col(ff_cols, half),
         stepped(half, 2 * ff_cols)],
        [shape_of((D, size), HALF), shape_of((size, D), HALF), shape_of((size, ff_cols), HALF),
         shape_of((ff_cols, size), HALF),
         shape_of((size, 2 * ff_cols), HALF)],
        (far(out_grad),) + tuple(far(piece) for piece in pieces) + (weights,),
        scratch=[pltpu.VMEM((half, D), HALF)],
        table=table,
        flops=2 * size * D * ff_cols * 3,
        after=after,
        room=12,
    )


def project_kernel(left_ref, right_ref, send_ref, keep_ref):
    put_halves(pl.program_id(0), 2, mul(left_ref[...], right_ref[...], NT), send_ref, keep_ref)


def project(left, weights, at, after, kept=shape_of):
    size, depth = left.shape
    half = size // 2
    return call(
        project_kernel,
        (2,),
        [stepped(half, depth), pl.BlockSpec((D, depth), lambda *_: (0, at))],
        halves_of(2, half, D),
        [shape_of((half, D), HALF), kept((half, D), FULL)],
        (left, weights),
        flops=2 * size * D * depth,
        after=after,
    )


def mid_kernel(tab_ref, x_ref, part_ref, other_ref, g_ref, resid_ref, h_ref):
    resid = x_ref[...] + (part_ref[...].astype(FULL) + other_ref[...].astype(FULL))
    resid_ref[...] = resid
    h_ref[...] = rms_parts(resid, g_ref[...])[0].astype(HALF)


def mid_back_kernel(tab_ref, grad_ref, part_ref, other_ref, g_ref, resid_ref, delta_ref, branch_ref, term_ref):
    d_h = part_ref[...].astype(FULL) + other_ref[...].astype(FULL)
    _, unit, factor = rms_parts(resid_ref[...], 1.0)
    delta = norm_back(d_h, unit, factor, g_ref[...])
    delta_ref[...] = delta
    branch_ref[...] = (grad_ref[...] + delta).astype(HALF)
    add_term(term_ref, d_h * unit)


def in_back_kernel(tab_ref, x_ref, part_ref, other_ref, g_ref, mid_ref, delta_ref, term_ref):
    d_h = part_ref[...].astype(FULL) + other_ref[...].astype(FULL)
    _, unit, factor = rms_parts(x_ref[...], 1.0)
    delta_ref[...] = (mid_ref[...] + norm_back(d_h, unit, factor, g_ref[...])).astype(HALF)
    add_term(term_ref, d_h * unit)


def add_term(term_ref, product):
    @pl.when(pl.program_id(0) == 0)
    def _():
        term_ref[...] = jnp.zeros(term_ref.shape, FULL)

    term_ref[...] += jnp.sum(product, axis=0, keepdims=True)


def norm_rows(kernel, own_half, base, part, other, gain, extra, kinds, with_term, after=()):
    half = part.shape[0]
    steps = half // ROWS
    rows = stepped(ROWS, D)
    return call(
        kernel,
        (steps,),
        [pl.BlockSpec((ROWS, D), lambda i, tab: (tab[0] * steps + i, 0)), rows, rows, whole(1, D)]
        + [rows] * len(extra),
        [rows] * len(kinds) + [made(1, D)] * with_term,
        [near_shape((half, D), dtype) if dtype == FULL else shape_of((half, D), dtype) for dtype in kinds] + [shape_of((1, D), FULL)] * with_term,
        (far(base), part, other, gain[None]) + tuple(near(item) for item in extra),
        table=own_half,
        after=after,
    )


def delta_kernel(a_ref, b_ref, c_ref, d_ref, out_ref):
    first = a_ref[...].astype(FULL) + b_ref[...].astype(FULL)
    out_ref[...] = (first + (c_ref[...].astype(FULL) + d_ref[...].astype(FULL))).astype(HALF)


def layer_delta(terms, after):
    rows = stepped(ROWS, D)
    half = terms[0].shape[0]
    return call(
        delta_kernel, (half // ROWS,), [rows] * 4, [rows], [shape_of((half, D), HALF)], terms, after=after
    )[0]


def stacked(values, order):
    high = values.astype(HALF).astype(FULL)
    low = values - high
    return jnp.concatenate([low if pick else high for pick in order], axis=0).astype(HALF)


def thin(factor, matrix, dims):
    result = mul(stacked(factor, (0, 1)), matrix.astype(HALF), dims)
    return result[:RANK] + result[RANK:]


def outer(left, right):
    return mul(stacked(left, (0, 0, 1, 1)), stacked(right, (0, 1, 0, 1)), TN)


def tile_of(size):
    return 256 if size % 256 == 0 else 128


def grad_kernel(flipped, thinned, lefts, rights, tab_ref, e_ref, f_ref, *refs):
    left_refs, right_refs, refs = refs[:lefts], refs[lefts : lefts + rights], refs[lefts + rights :]
    m_ref, right_scr = refs[0], refs[-1]
    depth = right_scr.shape[0] // rights
    for number, right in enumerate(right_refs):
        right_scr[number * depth : (number + 1) * depth, :] = right[...].astype(HALF)
    depth = right_scr.shape[0] // lefts
    total = e_ref[...]
    for number, left in enumerate(left_refs):
        total = total + mul(left[...], right_scr[number * depth : (number + 1) * depth, :])
    m_ref[...] = total
    p_ref = refs[1]
    if not thinned:
        p_ref[...] = jnp.zeros(p_ref.shape, FULL)
        return
    if flipped:
        p_ref[...] = thin(f_ref[...], total, NN)
    else:
        @pl.when(pl.program_id(0) == 0)
        def _():
            p_ref[...] = jnp.zeros(p_ref.shape, FULL)

        p_ref[...] += thin(f_ref[...], total, NT)


def merge_grad(table, lefts, rights, error, factor_t, flipped, thinned=True, after=()):
    height, width = error.shape
    tile = tile_of(width)
    by_col = lambda rows: pl.BlockSpec((rows, tile), lambda i, _: (0, i))
    rows = lefts[0][2] * len(lefts)
    depth = rows // len(rights)

    def left_spec(place, width):
        return pl.BlockSpec((height, width), lambda i, _: (0, place))

    def right_spec(place, given):
        return pl.BlockSpec((depth, tile), lambda i, tab: (tab[place] if given else place, i))

    p_shape = (RANK, width if flipped else height)
    p_spec = by_col(RANK) if flipped else made(*p_shape)
    if not thinned:
        p_shape = (RANK, 128)
        p_spec = made(*p_shape)
    return call(
        functools.partial(grad_kernel, flipped, thinned, len(lefts), len(rights)),
        (width // tile,),
        [by_col(height), whole(RANK, height) if flipped else by_col(RANK)]
        + [left_spec(place, size) for _, place, size in lefts]
        + [right_spec(place, given) for _, place, given in rights],
        [by_col(height), p_spec],
        [(far_shape if thinned else shape_of)((height, width), FULL), shape_of(p_shape, FULL)],
        (far(error), factor_t)
        + tuple(left[0] for left in lefts)
        + tuple(far(right[0]) if right[2] else right[0] for right in rights),
        scratch=[pltpu.VMEM((rows, tile), HALF)],
        table=table,
        flops=2 * height * width * rows,
        room=8,
        after=after,
    )


def error_kernel(e_ref, f_ref, p_ref):
    p_ref[...] = thin(f_ref[...], e_ref[...], NT)


def error_factor(error, factor_t, after):
    height, width = error.shape
    return call(
        error_kernel,
        (height // BLOCK,),
        [stepped(BLOCK, width), whole(RANK, width)],
        [stepped_col(RANK, BLOCK)],
        [shape_of((RANK, height), FULL)],
        (far(error), factor_t),
        after=after,
    )[0]


def first_kernel(e_ref, h_ref, *refs):
    p_ref = refs[-1]
    total, at = e_ref[...], 0
    for thin_ref in refs[:-1]:
        rows = thin_ref.shape[1]
        both = mul(stacked(thin_ref[...], (0, 1)), h_ref[:, at : at + rows], NT)
        total, at = total + both[:RANK] + both[RANK:], at + rows
    p_ref[...] = total


def first_factor(error_part, h_t, thins):
    return call(
        first_kernel,
        (1,),
        [whole(RANK, D), whole(*h_t.shape)] + [whole(*part.shape) for part in thins],
        [made(RANK, D)],
        [shape_of((RANK, D), FULL)],
        (error_part, h_t) + tuple(thins),
    )[0]


def orthonormal(block):
    rows = lax.broadcasted_iota(jnp.int32, block.shape, 0)
    for row_id in range(RANK):
        row = block[row_id : row_id + 1, :]
        inner = jnp.sum(block * row, axis=1, keepdims=True)
        inverse = lax.rsqrt(inner[row_id : row_id + 1, :] + 1e-12)
        finished = row * inverse
        later = block - (inner * inverse) * finished
        block = jnp.where(rows == row_id, finished, jnp.where(rows > row_id, later, block))
    return block


def second_kernel(flipped, workers, p_ref, m_ref, hat_ref, q_ref):
    step = pl.program_id(0)
    tile = m_ref.shape[0]

    @pl.when(step == 0)
    def _():
        hat_ref[...] = orthonormal(p_ref[...] / workers)
        if not flipped:
            q_ref[...] = jnp.zeros(q_ref.shape, FULL)

    if flipped:
        q_ref[...] = thin(hat_ref[...], m_ref[...], NT)
    else:
        q_ref[...] += thin(hat_ref[:, pl.ds(pl.multiple_of(step * tile, tile), tile)], m_ref[...], NN)


def second_factor(merged, p_sum, flipped, workers, after=()):
    height, width = merged.shape
    tile = tile_of(height)
    q_shape = (RANK, height if flipped else width)
    return call(
        functools.partial(second_kernel, flipped, workers),
        (height // tile,),
        [whole(RANK, D), pl.BlockSpec((tile, width), lambda i: (i, 0))],
        [made(RANK, D), pl.BlockSpec((RANK, tile), lambda i: (0, i)) if flipped else made(*q_shape)],
        [shape_of((RANK, D), FULL), shape_of(q_shape, FULL)],
        (p_sum, merged),
        flops=64 * height * width,
        after=after,
    )


def final_kernel(flipped, m_ref, hat_ref, q_ref, own_ref, moment_ref, weight_ref, err_ref, nw_ref, nm_ref):
    step = pl.program_id(0)
    tile = m_ref.shape[0]
    at = pl.ds(pl.multiple_of(step * tile, tile), tile)
    if flipped:
        err_ref[...] = m_ref[...] - outer(q_ref[:, at], hat_ref[...])
    else:
        err_ref[...] = m_ref[...] - outer(hat_ref[:, at], q_ref[...])

    @pl.when(step == 0)
    def _():
        if flipped:
            approx = outer(q_ref[...], own_ref[...])
        else:
            approx = outer(own_ref[...], q_ref[...])
        moment = MOMENTUM * moment_ref[...] + approx
        nm_ref[...] = moment
        nw_ref[...] = weight_ref[...] - STEP_RATE * moment


def final_update(merged, p_hat, q_new, p_own, moment, weight, flipped, after=()):
    height, width = merged.shape
    tile = tile_of(height)
    by_row = pl.BlockSpec((tile, width), lambda i: (i, 0))
    own, own_out = whole(*weight.shape), made(*weight.shape)
    return call(
        functools.partial(final_kernel, flipped),
        (height // tile,),
        [by_row, whole(*p_hat.shape), whole(*q_new.shape), whole(*p_own.shape), own, own],
        [by_row, own_out, own_out],
        [shape_of(merged.shape, FULL), shape_of(weight.shape, FULL), shape_of(weight.shape, FULL)],
        (merged, p_hat, q_new, p_own, moment, weight),
        flops=64 * height * width,
        after=after,
    )


def spread_kernel(tab_ref, base_ref, theirs_ref, mine_ref, *refs):
    out_ref, rows_scr, in_sems, out_sems = refs[-4:]
    half = theirs_ref.shape[0]
    count, block = rows_scr.shape[0], rows_scr.shape[1]
    each = half // block
    copies_in, copies_out = [], []
    for number in range(count):
        place = tab_ref[number // each] * half + number % each * block
        rows = pl.ds(pl.multiple_of(place, block), block)
        copies_in.append(pltpu.make_async_copy(base_ref.at[rows, :], rows_scr.at[number], in_sems.at[number]))
        copies_out.append(pltpu.make_async_copy(rows_scr.at[number], out_ref.at[rows, :], out_sems.at[number]))
        copies_in[number].start()
    for number in range(count):
        copies_in[number].wait()
        piece = theirs_ref if number < each else mine_ref
        at = number % each * block
        rows_scr[number] = rows_scr[number] + piece[at : at + block, :].astype(FULL)
        copies_out[number].start()
    for number in range(count):
        copies_out[number].wait()


def spread(table, base, pieces, before, after=()):
    half = pieces[0].shape[0]
    count = 2 * half // BLOCK
    extra = [] if before is None else [far(before)]
    anywhere = pl.BlockSpec(memory_space=pl.ANY)
    return call(
        spread_kernel,
        (1,),
        [anywhere, whole(half, D), whole(half, D)] + [anywhere] * len(extra),
        [anywhere],
        [far_shape(base.shape, FULL)],
        [far(base)] + list(pieces) + extra,
        scratch=[pltpu.VMEM((count, BLOCK, D), FULL), pltpu.SemaphoreType.DMA((count,)),
                 pltpu.SemaphoreType.DMA((count,))],
        table=table,
        aliases={4: 0} if extra else None,
        after=after,
    )[0]


def add_kernel(a_ref, b_ref, out_ref):
    out_ref[...] = a_ref[...] + b_ref[...]


def butterfly_step(values, axis, count, span, after=()):
    if span >= count:
        return values
    other = lax.ppermute(values, axis, [(i, i ^ span) for i in range(count)])
    spec = whole(*values.shape)
    return call(
        add_kernel, (1,), [spec, spec], [made(*values.shape)], [shape_of(values.shape, FULL)], (values, other), after=after
    )[0]


def to_core_mate(values, count):
    return lax.ppermute(values, "tensor", [(i, i ^ 1) for i in range(count)])


def chip_kernel(keep_ref, other_ref, out_ref):
    out_ref[...] = (keep_ref[...] + other_ref[...].astype(FULL)).astype(HALF)


def chip_sum(send, keep, count, after=()):
    rows = stepped(BLOCK, D)
    return call(
        chip_kernel, (send.shape[0] // BLOCK,), [rows, rows], [rows], [shape_of(send.shape, HALF)],
        (keep, to_core_mate(send, count)), after=after,
    )[0]


def across_chips(part, count):
    span = 2
    while True:
        other = lax.ppermute(part, "tensor", [(i, i ^ span) for i in range(count)])
        span *= 2
        if span >= count:
            return part, other
        part = (part.astype(FULL) + other.astype(FULL)).astype(HALF)


def pieces_of(own, count):
    return to_core_mate(own, count), own


def local(
    hidden_in,
    seg_ids,
    token_mask,
    out_grad,
    proj_qkv,
    proj_out,
    proj_gate_up,
    proj_down,
    gains,
    moment_qkv,
    moment_out,
    moment_gate_up,
    moment_down,
    error_qkv,
    error_out,
    error_gate_up,
    error_down,
    factor_qkv,
    factor_out,
    factor_gate_up,
    factor_down,
    gain_moment,
):
    parts = lax.axis_size("tensor")
    workers = lax.axis_size("dp")
    rows = hidden_in.shape[0]
    q_heads = QUERY_HEADS // parts
    kv_heads = KEY_VALUE_HEADS // parts
    group = QUERY_HEADS // KEY_VALUE_HEADS
    half = rows // CHUNKS // 2
    order = list(range(CHUNKS))[::-1]
    first_own = jnp.concatenate([proj_qkv, proj_out.T], axis=1).astype(HALF)
    second_own = jnp.concatenate([proj_gate_up, proj_down.T], axis=1).astype(HALF)
    first_pieces, first_steps = ring_gather(first_own, workers)
    shard_places = ring_places(workers, first_own.shape[0])
    g_att = gains[:D]
    g_mlp = gains[D : 2 * D]
    g_query = gains[2 * D : 2 * D + HEAD_SIZE]
    g_key = gains[2 * D + HEAD_SIZE :]
    cosine, sine = rope_tables(rows)

    core = lax.axis_index("tensor") % 2
    seg_row, seg_col = seg_ids, seg_ids[0][:, None]
    key_row = jnp.where(token_mask == 1, seg_ids, -1)
    key_col = key_row[0][:, None]
    starts = jnp.sum(
        (seg_ids[0][None, :] < seg_ids[0][::BLOCK][:, None]).astype(jnp.int32), axis=1
    ) // BLOCK
    tables, half_tables = [], []
    each = half // BLOCK
    for chunk in range(CHUNKS):
        places = [2 * chunk + 1 - core, 2 * chunk + core]
        half_tables.append(jnp.stack(places).astype(jnp.int32))
        numbers = jnp.stack([place * each + i for place in places for i in range(each)]).astype(jnp.int32)
        tables.append(jnp.concatenate([numbers, starts[numbers]]))
    all_halves = jnp.concatenate([half_tables[chunk] for chunk in order])

    own_half = [table[1:] for table in half_tables]

    factors_t = [factor.T for factor in (factor_qkv, factor_out, factor_gate_up, factor_down)]
    h_att = input_norm(hidden_in, g_att)
    first_b, queries, keys, values, keys_t, raw_q, raw_k = make_qkv(
        shard_places, h_att, first_pieces, g_query, g_key, cosine, sine, q_heads, kv_heads, ()
    )
    second_b = lax.all_gather(stage(second_own, first_steps[-1] + (far(cosine), far(sine), far(key_col), shard_places) + tuple(tables)), "dp", axis=0, tiled=True)

    att, att_t, log_total, att_sum = {}, {}, {}, {}
    after, arrived = (), ()
    for chunk in order:
        att[chunk], att_t[chunk], log_total[chunk] = attend(
            chunk, tables[chunk], queries, keys, values, seg_col, key_row, group, after
        )
        if chunk == order[-1]:
            error_part = error_factor(error_qkv[0], factors_t[0], (log_total[chunk],))
            h_t = turned(h_att, (error_part,))
            arrived = arrived + (far(h_t),)
        part = chip_sum(*project(att[chunk], near(first_b), 2, arrived), parts)
        after = (part,)
        att_sum[chunk] = across_chips(part, parts)
        arrived = att_sum[chunk][1:]

    two = [(chunk, place) for chunk in order for place in (0, 1)]
    size = 2 * half
    h_mlp_t, d_mlp, activ, activ_t, d_gu, mid_sum, mlp_part, mlp_sum = {}, {}, {}, {}, {}, {}, {}, {}
    resid, h_pieces = {}, {}
    arrived = ()
    for chunk in order:
        filled = () if chunk == order[0] else mlp_part[order[0]][:1]
        resid[chunk], h_own = norm_rows(
            mid_kernel, own_half[chunk], hidden_in, *att_sum[chunk], g_mlp, (), (FULL, HALF), 0, filled
        )
        h_pieces[chunk] = pieces_of(h_own, parts)
        h_mlp_t[chunk], d_mlp[chunk], activ[chunk], activ_t[chunk], d_gu[chunk] = feed_forward(
            half_tables[chunk], out_grad, far(second_b) if chunk == order[0] else second_b, h_pieces[chunk], after
        )
        if chunk == order[-1]:
            merged_down, p_down = merge_grad(
                all_halves,
                [(activ_t[other], 0, size) for other in order],
                [(d_mlp[other], 0, False) for other in order],
                error_down[0], factors_t[3], True,
            )
            arrived = arrived + (p_down,)
        summed = project(d_gu[chunk], second_b, 0, arrived)
        if chunk == order[0]:
            mlp_part[chunk] = project(activ[chunk], second_b, 2, summed[:1], far_shape)
        part = chip_sum(*summed, parts)
        after = (part,)
        mid_sum[chunk] = across_chips(part, parts)
        arrived = mid_sum[chunk][1:]

    merged_gu, p_gu = merge_grad(
        all_halves,
        [(h_mlp_t[chunk], 0, size) for chunk in order],
        [(d_gu[chunk], 0, False) for chunk in order],
        error_gate_up[0], factors_t[2], False, after=after,
    )
    after = (p_gu,)
    for chunk in order[1:]:
        mlp_part[chunk] = project(activ[chunk], second_b, 2, after, far_shape)
        after = mlp_part[chunk][:1]
    branch_pieces, mid_delta = {}, {}
    term_mlp = jnp.zeros((1, D), FULL)
    for chunk in order:
        mid_delta[chunk], d_branch, more = norm_rows(
            mid_back_kernel, own_half[chunk], out_grad, *mid_sum[chunk], g_mlp, (resid[chunk],), (FULL, HALF), 1,
            after if chunk == order[-1] else (),
        )
        term_mlp = term_mlp + more
        branch_pieces[chunk] = pieces_of(d_branch, parts)
    after = (d_branch,)
    mlp_sum[order[0]] = across_chips(chip_sum(*mlp_part[order[0]], parts, (p_gu,)), parts)
    d_raw, thins, in_sum = {}, {}, {}
    later = ()
    term_q, term_k = (jnp.zeros((1, HEAD_SIZE), FULL) for _ in range(2))
    deltas = {}
    arrived = ()
    for chunk in order:
        raw_q_back, more_q, d_keys, d_values = attend_back(
            chunk, tables[chunk], queries, keys, values, keys_t, seg_row, key_col, first_b, att[chunk],
            log_total[chunk], raw_q, g_query, cosine, sine, branch_pieces[chunk], later, group, after
        )
        later = (d_keys, d_values)
        if chunk == order[0]:
            deltas[chunk] = layer_delta(att_sum[chunk] + mlp_sum[chunk], later)
            arrived = (deltas[chunk],)
        d_raw[chunk], thins[chunk], more_k, send, keep = raw_back(
            chunk, half_tables[chunk], raw_q_back, d_keys, d_values, raw_k, g_key, cosine, sine, first_b,
            factors_t[0], arrived
        )
        term_q, term_k = term_q + more_q, term_k + more_k
        part = chip_sum(send, keep, parts)
        after = (part,)
        in_sum[chunk] = across_chips(part, parts)
        arrived = in_sum[chunk][1:]
        if chunk == order[0]:
            merged_out, p_out = merge_grad(
                all_halves,
                [(att_t[other], 0, size) for other in order],
                [(branch_pieces[other][place], 0, False) for other, place in two],
                error_out[0], factors_t[1], True, after=after,
            )
            after = (p_out,)

    p_qkv = first_factor(error_part, h_t, [thins[chunk] for chunk in range(CHUNKS)])
    for chunk in order[1:]:
        mlp_sum[chunk] = across_chips(chip_sum(*mlp_part[chunk], parts, after), parts)
    after = after + (p_qkv,)
    term_att = jnp.zeros((1, D), FULL)
    in_delta = {}
    for chunk in order[:-1]:
        in_delta[chunk], more = norm_rows(
            in_back_kernel, own_half[chunk], hidden_in, *in_sum[chunk], g_att, (mid_delta[chunk],), (HALF,), 1, after
        )
        term_att = term_att + more
    p_all = jnp.concatenate([p_down, p_gu, p_out, p_qkv], axis=1)
    p_all = butterfly_step(p_all, "dp", workers, 1, tuple(in_delta.values()))
    merged_qkv, token = merge_grad(
        all_halves,
        [(h_t, chunk, size) for chunk in order],
        [(d_raw[chunk], 0, False) for chunk in order],
        error_qkv[0], factors_t[0], False, False, (p_all,),
    )
    p_all = butterfly_step(p_all, "dp", workers, 2, (token,))
    layer_out = spread(
        half_tables[order[0]], hidden_in, pieces_of(deltas[order[0]], parts), None, (p_all,)
    )
    p_all = butterfly_step(p_all, "dp", workers, 4, (far(layer_out),))
    p_all = butterfly_step(p_all, "dp", workers, 8)
    in_delta[order[-1]], more = norm_rows(
        in_back_kernel, own_half[order[-1]], hidden_in, *in_sum[order[-1]], g_att, (mid_delta[order[-1]],), (HALF,),
        1, (p_all,),
    )
    term_att = term_att + more
    hat_down, q_down = second_factor(merged_down, p_all[:, :D], True, workers)
    hat_gu, q_gu = second_factor(merged_gu, p_all[:, D : 2 * D], False, workers)
    hat_out, q_out = second_factor(merged_out, p_all[:, 2 * D : 3 * D], True, workers)
    hat_qkv, q_qkv = second_factor(merged_qkv, p_all[:, 3 * D :], False, workers)
    share = 2.0 / parts
    gain_terms = jnp.concatenate(
        [term_att[0] * share, term_mlp[0] * share, term_q[0], term_k[0]]
    ).reshape(RANK, -1)
    q_all = jnp.concatenate([q_down, q_gu, q_out, q_qkv, gain_terms], axis=1)
    cuts = [0]
    for part in (q_down, q_gu, q_out, q_qkv, gain_terms):
        cuts.append(cuts[-1] + part.shape[1])
    after = (q_down, q_gu, q_out, q_qkv)
    input_grad = spread(
        half_tables[order[0]], out_grad, pieces_of(in_delta[order[0]], parts), None, after
    )
    q_all = butterfly_step(q_all, "dp", workers, 1, (far(input_grad),))
    for chunk in order[1:]:
        deltas[chunk] = layer_delta(att_sum[chunk] + mlp_sum[chunk], (q_all,))
    q_all = butterfly_step(q_all, "dp", workers, 2, (deltas[order[-1]],))
    for chunk in order[1:]:
        input_grad = spread(
            half_tables[chunk], out_grad, pieces_of(in_delta[chunk], parts), input_grad, (q_all,)
        )
    q_all = butterfly_step(q_all, "dp", workers, 4, (far(input_grad),))
    q_all = butterfly_step(q_all, "dp", workers, 8) / workers
    for chunk in order[1:]:
        layer_out = spread(half_tables[chunk], hidden_in, pieces_of(deltas[chunk], parts), layer_out)
    gain_grad = q_all[:, cuts[4] :]
    for span in (1, 2, 4):
        gain_grad = butterfly_step(gain_grad, "tensor", parts, span)
    new_gain_moment = MOMENTUM * gain_moment + gain_grad.reshape(-1)
    new_gains = gains - GAIN_RATE * new_gain_moment

    own_count = D // workers
    results = {}
    for number, (name, merged, p_hat, moment, weight, flipped) in enumerate((
        ("down", merged_down, hat_down, moment_down, proj_down, True),
        ("gu", merged_gu, hat_gu, moment_gate_up, proj_gate_up, False),
        ("out", merged_out, hat_out, moment_out, proj_out, True),
        ("qkv", merged_qkv, hat_qkv, moment_qkv, proj_qkv, False),
    )):
        q_new = q_all[:, cuts[number] : cuts[number + 1]]
        p_own = lax.dynamic_slice_in_dim(p_hat, lax.axis_index("dp") * own_count, own_count, 1)
        new_error, new_weight, new_moment = final_update(
            merged, p_hat, q_new, p_own, moment, weight, flipped
        )
        results[name] = (new_weight, new_moment, new_error[None], q_new.T)
    ordered = [results[name] for name in ("qkv", "out", "gu", "down")]
    return (
        (layer_out, input_grad)
        + tuple(r[0] for r in ordered)
        + tuple(r[1] for r in ordered)
        + tuple(r[2] for r in ordered)
        + tuple(r[3] for r in ordered)
        + (new_gains, new_gain_moment)
    )


def solution(mesh):
    in_specs = (
        P("dp", None),
        P("dp", None),
        P("dp", None),
        P("dp", None),
        P("dp", "tensor"),
        P("tensor", "dp"),
        P("dp", "tensor"),
        P("tensor", "dp"),
        P(),
        P("dp", "tensor"),
        P("tensor", "dp"),
        P("dp", "tensor"),
        P("tensor", "dp"),
        P("dp", None, "tensor"),
        P("dp", "tensor", None),
        P("dp", None, "tensor"),
        P("dp", "tensor", None),
        P("tensor", None),
        P("tensor", None),
        P("tensor", None),
        P("tensor", None),
        P(),
    )
    out_specs = (
        P("dp", None),
        P("dp", None),
        P("dp", "tensor"),
        P("tensor", "dp"),
        P("dp", "tensor"),
        P("tensor", "dp"),
        P("dp", "tensor"),
        P("tensor", "dp"),
        P("dp", "tensor"),
        P("tensor", "dp"),
        P("dp", None, "tensor"),
        P("dp", "tensor", None),
        P("dp", None, "tensor"),
        P("dp", "tensor", None),
        P("tensor", None),
        P("tensor", None),
        P("tensor", None),
        P("tensor", None),
        P(),
        P(),
    )
    return jax.shard_map(local, mesh=mesh, in_specs=in_specs, out_specs=out_specs, check_vma=False)
```
